256 devices in a mesh: dp: 32 (over x_hi, z, core), node: 8 (over x_lo, y).
Axes of the slice: x: 4 (x_hi: 2, x_lo: 2; x = x_hi * 2 + x_lo), y: 4, z: 8, core: 2. Of those that a mesh axis runs over, the one named last changes fastest.
Arguments:
- hidden: bfloat16 [131072, 1024], P(('dp', 'node')), may hold values from -6 to 6
- norm_gain: float32 [1024], replicated, may hold values from 0.1 to 1.9
- w_query: bfloat16 [1024, 1024], P('node', 'dp'), may hold values from -0.1875 to 0.1875
- w_key: bfloat16 [1024, 256], P('node', 'dp'), may hold values from -0.1875 to 0.1875
- w_value: bfloat16 [1024, 256], P('node', 'dp'), may hold values from -0.1875 to 0.1875
- w_out: bfloat16 [1024, 1024], P('node', 'dp'), may hold values from -0.1875 to 0.1875
- doc_lengths: int32 [512, 4], P(('dp', 'node')), may hold values from 1 to 128, 256 in all within a row
- cotangent: bfloat16 [131072, 1024], P(('dp', 'node')), may hold values from -24 to 24
Outputs:
- output: bfloat16 [131072, 1024], P(('dp', 'node'))
- grad_hidden: bfloat16 [131072, 1024], P(('dp', 'node'))
- grad_query: float32 [1024, 1024], P('node', 'dp')
- grad_key: float32 [1024, 256], P('node', 'dp')
- grad_value: float32 [1024, 256], P('node', 'dp')
- grad_out: float32 [1024, 1024], P('node', 'dp')
The draws below stay inside these ranges and needn't reach their ends.
Inputs may be any that keep to these rules, and one draw needn't show every extreme that they name: `doc_lengths`: each row holds the lengths of 4 documents that fill one sequence of 256 tokens; the longest is exactly half of 256.
All inputs are finite; a program needn't handle non-finite values.
Results may differ from the reference program's by a relative error of at most 0.0098.
Values may be sent and summed in bfloat16 or wider, within the bound.
No kernel may reach another device: no remote copies, remote signals or barrier semaphores. Data moves between devices by JAX's collectives and lax.ppermute only.
A program may use at most 128 MiB of HBM per device.

```python
import math
import jax
import jax.numpy as jnp
import numpy as np
from jax import lax

D = 1024
QH = 16
KVH = 4
HD = 64
SEQ_LEN = 256
DOCS = 4
SEQS = 512
TOKENS = 131072


def raised(result, rng, source, target, blocks, factor):
    def block_of(dim):
        return (jnp.arange(result.shape[dim]) // (result.shape[dim] // blocks)).reshape((-1,) + (1,) * (result.ndim - 1 - dim))

    one_side = jax.random.permutation(rng, blocks)[block_of(target)]
    far = (block_of(target) + blocks // 2) % blocks
    return jnp.where((block_of(source) == one_side) | (block_of(source) == far), factor * result, result)


def levels(stream_key, shape, shards, smallest, top_value):
    def one(position, parts):
        draws = jax.random.uniform(jax.random.fold_in(jax.random.fold_in(stream_key, 6), position), (parts,), jnp.float32, smallest / len(shards), top_value / len(shards))
        return jnp.repeat(jnp.exp(draws), shape[position] // parts).reshape((-1,) + (1,) * (len(shape) - position - 1))

    gain = one(*shards[0])
    for cut in shards[1:]:
        gain = gain * one(*cut)
    return gain


def profile(count, total, most, slope):
    portions = [(1 << 20) // math.isqrt(standing ** slope) + 1 for standing in range(2, count + 1)]
    spare, holding = total - most - (count - 1), [1] * (count - 1)
    while spare > 0:
        movable = [i for i in range(count - 1) if holding[i] < most]
        mass, remaining = sum([portions[i] for i in movable]), spare
        for i in movable:
            addition = min(most - holding[i], max(1, remaining * portions[i] // mass), spare)
            holding[i] = holding[i] + addition
            spare = spare - addition
    return np.array([most] + holding)


def ragged_sizes(own_key, count, total, bound, slope):
    if count == 2:
        one = jax.random.randint(own_key, (), max(1, total - bound), min(bound, total - 1) + 1)
        return jnp.stack([one, total - one])
    lengths = jnp.asarray(profile(count, total, bound, slope), jnp.int32)
    pairs = (count - 1) // 2
    giver, receiver = lengths[1:1 + 2 * pairs:2], lengths[2:2 + 2 * pairs:2]
    slack = jnp.minimum(giver - 1, bound - receiver)
    shifted = jax.random.randint(jax.random.fold_in(own_key, 1), (pairs,), 0, 1 << 20) % (slack + 1)
    lengths = lengths.at[1:1 + 2 * pairs:2].set(giver - shifted).at[2:2 + 2 * pairs:2].set(receiver + shifted)
    return lengths[jax.random.permutation(jax.random.fold_in(own_key, 2), count)]


def gaussian(stream_key, extent, scale, bound, cuts=(), held_as=jnp.bfloat16):
    values = jax.random.normal(stream_key, extent, jnp.float32) * scale
    if len(cuts) > 0:
        values = levels(stream_key, extent, cuts, -0.22, 0.18) * values
    return jnp.clip(values, min=-bound, max=bound).astype(held_as)


def heavy_noise(own_key, dims, deviation, reach, split, heavy, held_as=jnp.bfloat16):
    entries = deviation * jax.random.normal(own_key, dims, jnp.float32)
    if split:
        entries = entries * levels(own_key, dims, split, -0.22, 0.18)
    return jnp.clip(raised(entries, jax.random.fold_in(own_key, 3), *heavy), -reach, reach).astype(held_as)


def setup_inputs(seed: int = 0) -> dict:
    key_list = jax.random.split(jax.random.key(seed), 9)
    hidden = gaussian(key_list[0], (TOKENS, D), 1.0, 6.0, ((0, 256),))
    norm_gain = jnp.clip(1.0 + 0.18 * jax.random.normal(key_list[1], (D,), jnp.float32), 0.1, 1.9)
    w_query = gaussian(key_list[2], (D, QH * HD), D ** -0.5, 0.1875, ((0, 8), (1, 32)))
    w_key = gaussian(key_list[3], (D, KVH * HD), D ** -0.5, 0.1875, ((0, 8), (1, 32)))
    w_value = gaussian(key_list[4], (D, KVH * HD), D ** -0.5, 0.1875, ((0, 8), (1, 32)))
    w_out = gaussian(key_list[5], (QH * HD, D), (QH * HD) ** -0.5, 0.1875, ((0, 8), (1, 32)))
    doc_lengths = jax.vmap(lambda own: ragged_sizes(own, DOCS, SEQ_LEN, SEQ_LEN // 2, 1))(jax.random.split(key_list[6], SEQS)).reshape((SEQS, DOCS)).astype(jnp.int32)
    cotangent = heavy_noise(key_list[7], (TOKENS, D), 1.0, 24.0, ((0, 256),), (0, 1, 256, 6.0))
    return dict(hidden=hidden, norm_gain=norm_gain, w_query=w_query, w_key=w_key, w_value=w_value, w_out=w_out, doc_lengths=doc_lengths, cotangent=cotangent)


def rotary(length, head_dim):
    halfway = head_dim // 2
    frequency = 500000.0 ** (-2.0 * jnp.arange(halfway, dtype=jnp.float32) / head_dim)
    angles = jnp.arange(length, dtype=jnp.float32)[:, None] * frequency[None, :]
    return (jnp.cos(angles), jnp.sin(angles))

def rotate(tensor, cosine, sine_part, direction):
    halfway = tensor.shape[-1] // 2
    first = tensor[..., :halfway]
    second = tensor[..., halfway:]
    across = cosine[:, None, :]
    upward = direction * sine_part[:, None, :]
    return jnp.concatenate([first * across - second * upward, first * upward + second * across], axis=-1)

def doc_allowed(doc_lengths, length):
    bounds = jnp.cumsum(doc_lengths, axis=-1)
    places = jnp.arange(length, dtype=jnp.int32)
    segment = lax.optimization_barrier(jnp.sum((places[:, None] >= bounds[..., None, :]).astype(jnp.int32), axis=-1))
    same_doc = segment[..., :, None] == segment[..., None, :]
    causal = places[:, None] >= places[None, :]
    return jnp.logical_and(same_doc, causal)

def sequence_step(hidden, cotangent, doc_lengths, norm_gain, w_query, w_key, w_value, w_out):
    length = hidden.shape[0]
    q_heads = w_query.shape[1] // HD
    kv_heads = w_key.shape[1] // HD
    group_size = q_heads // kv_heads
    scale = HD ** (-0.5)
    cosine, sine_part = rotary(length, HD)
    allowed = doc_allowed(doc_lengths, length)
    rows = hidden.astype(jnp.float32)
    inverse = lax.rsqrt(lax.optimization_barrier(jnp.mean(rows * rows, axis=-1, keepdims=True)) + 1e-05)
    unit_rows = rows * inverse
    normed = (unit_rows * norm_gain).astype(jnp.bfloat16)
    query_rot = rotate(jnp.dot(normed, w_query, preferred_element_type=jnp.float32).reshape(length, q_heads, HD), cosine, sine_part, 1.0).astype(jnp.bfloat16)
    key_rot = rotate(jnp.dot(normed, w_key, preferred_element_type=jnp.float32).reshape(length, kv_heads, HD), cosine, sine_part, 1.0).astype(jnp.bfloat16)
    value_rows = jnp.dot(normed, w_value, preferred_element_type=jnp.float32).astype(jnp.bfloat16)
    grouped = query_rot.reshape(length, kv_heads, group_size, HD).astype(jnp.float32)
    key_heads = key_rot.astype(jnp.float32)
    value_heads = value_rows.reshape(length, kv_heads, HD).astype(jnp.float32)
    scores = jnp.einsum('qkgd,skd->kgqs', grouped, key_heads) * scale
    raw_weights = jnp.where(allowed, jnp.exp(scores), 0.0)
    probability = raw_weights / lax.optimization_barrier(jnp.sum(raw_weights, axis=-1, keepdims=True))
    prob_bf = probability.astype(jnp.bfloat16).astype(jnp.float32)
    mixed = jnp.einsum('kgqs,skd->qkgd', prob_bf, value_heads).reshape(length, q_heads * HD).astype(jnp.bfloat16)
    output = (rows + jnp.dot(mixed, w_out, preferred_element_type=jnp.float32)).astype(jnp.bfloat16)
    grad_out = jnp.dot(mixed.T, cotangent, preferred_element_type=jnp.float32)
    d_mixed = jnp.dot(cotangent, w_out.T, preferred_element_type=jnp.float32).astype(jnp.bfloat16)
    mixed_heads = d_mixed.reshape(length, kv_heads, group_size, HD).astype(jnp.float32)
    d_prob = jnp.einsum('qkgd,skd->kgqs', mixed_heads, value_heads)
    inner = lax.optimization_barrier(jnp.sum(probability * d_prob, axis=-1, keepdims=True))
    d_score = (probability * (d_prob - inner) * scale).astype(jnp.bfloat16).astype(jnp.float32)
    query_back = jnp.einsum('kgqs,skd->qkgd', d_score, key_heads).reshape(length, q_heads, HD)
    d_query = rotate(query_back, cosine, sine_part, -1.0).reshape(length, q_heads * HD).astype(jnp.bfloat16)
    key_back = jnp.einsum('kgqs,qkgd->skd', d_score, grouped)
    d_key = rotate(key_back, cosine, sine_part, -1.0).reshape(length, kv_heads * HD).astype(jnp.bfloat16)
    d_value = jnp.einsum('kgqs,qkgd->skd', prob_bf, mixed_heads).reshape(length, kv_heads * HD).astype(jnp.bfloat16)
    grad_query = jnp.dot(normed.T, d_query, preferred_element_type=jnp.float32)
    grad_key = jnp.dot(normed.T, d_key, preferred_element_type=jnp.float32)
    grad_value = jnp.dot(normed.T, d_value, preferred_element_type=jnp.float32)
    d_normed = jnp.dot(d_query, w_query.T, preferred_element_type=jnp.float32)
    d_normed = d_normed + jnp.dot(d_key, w_key.T, preferred_element_type=jnp.float32)
    d_normed = d_normed + jnp.dot(d_value, w_value.T, preferred_element_type=jnp.float32)
    d_unit = d_normed * norm_gain
    grad_hidden = (cotangent.astype(jnp.float32) + inverse * (d_unit - unit_rows * lax.optimization_barrier(jnp.mean(d_unit * unit_rows, axis=-1, keepdims=True)))).astype(jnp.bfloat16)
    return (output, grad_hidden, (grad_query, grad_key, grad_value, grad_out))

def reference(hidden, norm_gain, w_query, w_key, w_value, w_out, doc_lengths, cotangent):
    sequences = hidden.reshape(-1, SEQ_LEN, D)
    cot_rows = cotangent.reshape(-1, SEQ_LEN, D)
    starting = (jnp.zeros(w_query.shape, jnp.float32), jnp.zeros(w_key.shape, jnp.float32), jnp.zeros(w_value.shape, jnp.float32), jnp.zeros(w_out.shape, jnp.float32))

    def advance(totals, slices):
        output, grad_hidden, grads = sequence_step(slices[0], slices[1], slices[2], norm_gain, w_query, w_key, w_value, w_out)
        return (tuple((total + grad for total, grad in zip(totals, grads))), (output, grad_hidden))
    totals, stacked = lax.scan(advance, starting, (sequences, cot_rows, doc_lengths))
    output = stacked[0].reshape(-1, D)
    grad_hidden = stacked[1].reshape(-1, D)
    return (output, grad_hidden, totals[0], totals[1], totals[2], totals[3])
```

```python
import jax
import jax.numpy as jnp
from jax import lax
from jax.sharding import PartitionSpec as P

HD = 64
SEQ_LEN = 256


def rotary(length, head_dim):
    halfway = head_dim // 2
    frequency = 500000.0 ** (-2.0 * jnp.arange(halfway, dtype=jnp.float32) / head_dim)
    angles = jnp.arange(length, dtype=jnp.float32)[:, None] * frequency[None, :]
    return (jnp.cos(angles), jnp.sin(angles))


def rotate(tensor, cosine, sine_part, direction):
    halfway = tensor.shape[-1] // 2
    first = tensor[..., :halfway]
    second = tensor[..., halfway:]
    across = cosine[:, None, :]
    upward = direction * sine_part[:, None, :]
    return jnp.concatenate(
        [first * across - second * upward, first * upward + second * across], axis=-1
    )


def doc_allowed(doc_lengths, length):
    bounds = jnp.cumsum(doc_lengths, axis=-1)
    places = jnp.arange(length, dtype=jnp.int32)
    segment = jnp.sum((places[:, None] >= bounds[..., None, :]).astype(jnp.int32), axis=-1)
    same_doc = segment[..., :, None] == segment[..., None, :]
    causal = places[:, None] >= places[None, :]
    return jnp.logical_and(same_doc, causal)


def token_sum(left, right):
    return jnp.einsum("td,tf->df", left, right, preferred_element_type=jnp.float32)


AXES = ("xh", "z", "c", "xl", "y")
SIZES = (2, 8, 2, 2, 4)


def shift(block, axis, size, step):
    return lax.ppermute(block, axis, [(i, (i - step) % size) for i in range(size)])


def swap(block, axis):
    return lax.ppermute(block, axis, [(0, 1), (1, 0)])


def gather_blocks(block):
    mine = lax.all_to_all(
        jnp.broadcast_to(block[None], (16,) + block.shape), ("xh", "z"), 0, 0, tiled=True
    )
    own = jnp.stack([mine, swap(mine, "xl")])
    round_y = [own, shift(own, "y", 4, 1), shift(own, "y", 4, 2), shift(own, "y", 4, 3)]
    return [round_y, [swap(part, "c") for part in round_y]]


def scatter_blocks(keep, send):
    f32 = jnp.float32
    summed = []
    for step in range(4):
        arrived = swap(send[step], "c")
        summed.append((keep[step].astype(f32) + arrived.astype(f32)).astype(jnp.bfloat16))
    arrived = [shift(summed[step], "y", 4, -step) for step in (1, 2, 3)]
    total = summed[0].astype(f32) + sum(part.astype(f32) for part in arrived)
    total = total.astype(jnp.bfloat16)
    pair = (total[0].astype(f32) + swap(total[1], "xl").astype(f32)).astype(jnp.bfloat16)
    parts = lax.all_to_all(pair, ("xh", "z"), 0, 0, tiled=True)
    return jnp.sum(parts.astype(f32), axis=0)


def pack(w_query, w_key, w_value, w_out):
    return jnp.concatenate([w_query.T, w_key.T, w_value.T, w_out.T], axis=0)


def whole(blocks):
    c, xl, y = (lax.axis_index(name) for name in ("c", "xl", "y"))
    every = jnp.stack([jnp.stack(row) for row in blocks])
    every = jnp.take(every, (jnp.arange(2) - c) % 2, axis=0)
    every = jnp.take(every, (jnp.arange(4) - y) % 4, axis=1)
    every = jnp.take(every, (jnp.arange(2) - xl) % 2, axis=2)
    every = every.transpose(2, 1, 5, 3, 0, 4)
    every = every.reshape(1024, 32, 80)
    return (
        every[..., :32].reshape(1024, 1024),
        every[..., 32:40].reshape(1024, 256),
        every[..., 40:48].reshape(1024, 256),
        every[..., 48:].reshape(1024, 1024),
    )


def spread(terms):
    c, xl, y = (lax.axis_index(name) for name in ("c", "xl", "y"))
    every = jnp.concatenate(
        [term.astype(jnp.bfloat16).reshape(1024, 32, -1) for term in terms], axis=-1
    )
    every = every.reshape(2, 4, 128, 16, 2, 80).transpose(4, 1, 0, 3, 5, 2)
    every = jnp.take(every, (jnp.arange(2) + c) % 2, axis=0)
    every = jnp.take(every, (jnp.arange(4) + y) % 4, axis=1)
    return jnp.take(every, (jnp.arange(2) + xl) % 2, axis=2)


def local(hidden, norm_gain, w_query, w_key, w_value, w_out, doc_lengths, cotangent):
    blocks = gather_blocks(pack(w_query, w_key, w_value, w_out))
    query_full, key_full, value_full, out_full = whole(blocks)
    batch = doc_lengths.shape[0]
    length = SEQ_LEN
    q_heads = query_full.shape[1] // HD
    kv_heads = key_full.shape[1] // HD
    group_size = q_heads // kv_heads
    scale = HD ** (-0.5)
    cosine, sine_part = rotary(length, HD)
    allowed = doc_allowed(doc_lengths, length)[:, None, None]
    rows = hidden.astype(jnp.float32)
    inverse = lax.rsqrt(jnp.mean(rows * rows, axis=-1, keepdims=True) + 1e-05)
    unit_rows = rows * inverse
    normed = (unit_rows * norm_gain).astype(jnp.bfloat16)
    query_proj = jnp.dot(normed, query_full, preferred_element_type=jnp.float32).reshape(
        batch, length, q_heads, HD
    )
    key_proj = jnp.dot(normed, key_full, preferred_element_type=jnp.float32).reshape(
        batch, length, kv_heads, HD
    )
    query_rot = rotate(query_proj, cosine, sine_part, 1.0).astype(jnp.bfloat16)
    key_rot = rotate(key_proj, cosine, sine_part, 1.0).astype(jnp.bfloat16)
    value_rows = jnp.dot(normed, value_full, preferred_element_type=jnp.float32).astype(
        jnp.bfloat16
    )
    grouped = query_rot.reshape(batch, length, kv_heads, group_size, HD)
    value_heads = value_rows.reshape(batch, length, kv_heads, HD)
    scores = (
        jnp.einsum("bqkgd,bskd->bkgqs", grouped, key_rot, preferred_element_type=jnp.float32)
        * scale
    )
    raw_weights = jnp.where(allowed, jnp.exp(scores), 0.0)
    probability = raw_weights / jnp.sum(raw_weights, axis=-1, keepdims=True)
    prob_bf = probability.astype(jnp.bfloat16)
    mixed = jnp.einsum(
        "bkgqs,bskd->bqkgd", prob_bf, value_heads, preferred_element_type=jnp.float32
    )
    mixed = mixed.reshape(batch * length, q_heads * HD).astype(jnp.bfloat16)
    output = (rows + jnp.dot(mixed, out_full, preferred_element_type=jnp.float32)).astype(
        jnp.bfloat16
    )
    term_out = token_sum(mixed, cotangent)
    d_mixed = jnp.einsum(
        "tf,df->td", cotangent, out_full, preferred_element_type=jnp.float32
    ).astype(jnp.bfloat16)
    mixed_heads = d_mixed.reshape(batch, length, kv_heads, group_size, HD)
    d_prob = jnp.einsum(
        "bqkgd,bskd->bkgqs", mixed_heads, value_heads, preferred_element_type=jnp.float32
    )
    inner = jnp.sum(probability * d_prob, axis=-1, keepdims=True)
    d_score = (probability * (d_prob - inner) * scale).astype(jnp.bfloat16)
    query_grad_rot = jnp.einsum(
        "bkgqs,bskd->bqkgd", d_score, key_rot, preferred_element_type=jnp.float32
    )
    query_grad_rot = query_grad_rot.reshape(batch, length, q_heads, HD)
    d_query = (
        rotate(query_grad_rot, cosine, sine_part, -1.0)
        .reshape(batch * length, q_heads * HD)
        .astype(jnp.bfloat16)
    )
    key_grad_rot = jnp.einsum(
        "bkgqs,bqkgd->bskd", d_score, grouped, preferred_element_type=jnp.float32
    )
    d_key = (
        rotate(key_grad_rot, cosine, sine_part, -1.0)
        .reshape(batch * length, kv_heads * HD)
        .astype(jnp.bfloat16)
    )
    d_value = jnp.einsum(
        "bkgqs,bqkgd->bskd", prob_bf, mixed_heads, preferred_element_type=jnp.float32
    )
    d_value = d_value.reshape(batch * length, kv_heads * HD).astype(jnp.bfloat16)
    term_query = token_sum(normed, d_query)
    term_key = token_sum(normed, d_key)
    term_value = token_sum(normed, d_value)
    d_normed = jnp.einsum("tf,df->td", d_query, query_full, preferred_element_type=jnp.float32)
    d_normed = d_normed + jnp.einsum(
        "tf,df->td", d_key, key_full, preferred_element_type=jnp.float32
    )
    d_normed = d_normed + jnp.einsum(
        "tf,df->td", d_value, value_full, preferred_element_type=jnp.float32
    )
    d_unit = d_normed * norm_gain
    grad_hidden = (
        cotangent.astype(jnp.float32)
        + inverse * (d_unit - unit_rows * jnp.mean(d_unit * unit_rows, axis=-1, keepdims=True))
    ).astype(jnp.bfloat16)
    terms = (term_query, term_key, term_value, term_out)
    every = spread(terms)
    owned = scatter_blocks(every[0], every[1])
    return (
        output,
        grad_hidden,
        owned[:32].T,
        owned[32:40].T,
        owned[40:48].T,
        owned[48:].T,
    )


def solution(mesh):
    wide = jax.sharding.Mesh(mesh.devices.reshape(SIZES), AXES)
    dp, node = ("xh", "z", "c"), ("xl", "y")
    tokens, weight = P(AXES, None), P(node, dp)
    return jax.shard_map(
        local,
        mesh=wide,
        in_specs=(tokens, P(), weight, weight, weight, weight, tokens, tokens),
        out_specs=(tokens, tokens, weight, weight, weight, weight),
        check_vma=False,
    )
```

```python
import functools

import jax
import jax.numpy as jnp
import numpy as np
from jax import lax
from jax.experimental import pallas as pl
from jax.experimental.pallas import tpu as pltpu
from jax.sharding import PartitionSpec as P

HD = 64
HALF = 32
SEQ = 256
D = 1024
KV = 256
GROUP = 4
TOKENS = 512

AXES = ("xh", "z", "c", "xl", "y")
SIZES = (2, 8, 2, 2, 4)
CHIPS = 16
ROWS = 80
BF = jnp.bfloat16
F32 = jnp.float32
VMEM_BYTES = 48 * 1024 * 1024
BLOCKED = -1e30


def tables():
    frequency = 500000.0 ** (-2.0 * np.arange(HALF) / HD)
    angles = np.tile(np.arange(SEQ), TOKENS // SEQ)[None, :] * frequency[:, None]
    return np.stack([np.cos(angles), np.sin(angles)]).astype(np.float32)


def dot(left, right):
    return jnp.dot(left, right, preferred_element_type=F32)


def shift(block, axis, size, step):
    return lax.ppermute(block, axis, [(i, (i - step) % size) for i in range(size)])


def swap(block, axis):
    return lax.ppermute(block, axis, [(0, 1), (1, 0)])


def gather_blocks(block):
    mine = lax.all_to_all(
        jnp.broadcast_to(block[None], (CHIPS, ROWS, 128)), ("xh", "z"), 0, 0, tiled=True
    )
    own = jnp.stack([mine, swap(mine, "xl")])
    pieces = [own, shift(own, "y", 4, 1), shift(own, "y", 4, 2), shift(own, "y", 4, 3)]
    return pieces + [swap(piece, "c") for piece in pieces]


def scatter_blocks(pieces):
    summed = []
    for step in range(4):
        arrived = swap(pieces[4 + step], "c")
        summed.append((pieces[step].astype(F32) + arrived.astype(F32)).astype(BF))
    total = summed[0].astype(F32)
    for step in (1, 2, 3):
        total = total + shift(summed[step], "y", 4, -step).astype(F32)
    total = total.astype(BF)
    pair = (total[0].astype(F32) + swap(total[1], "xl").astype(F32)).astype(BF)
    parts = lax.all_to_all(pair, ("xh", "z"), 0, 0, tiled=True)
    return jnp.sum(parts.astype(F32), axis=0)


def assembly(where, pieces, w_q, w_kv, w_o, sems):
    c, xl, y = where[0], where[1], where[2]
    copies = ([], [], [])
    for at in range(16):
        c_rel, y_rel, xl_rel = at // 8, (at // 2) % 4, at % 2
        source = pieces[c_rel * 4 + y_rel].at[xl_rel]
        core = lax.rem(c + c_rel, 2)
        node = lax.rem(xl + xl_rel, 2) * 4 + lax.rem(y + y_rel, 4)
        lanes = pl.ds(pl.multiple_of(node * 128, 128), 128)
        for part, (target, start, count) in enumerate(
            ((w_q, 0, 32), (w_kv, 32, 16), (w_o, 48, 32))
        ):
            copies[part].append(
                pltpu.make_async_copy(
                    source.at[:, pl.ds(start, count), :],
                    target.at[:, core, :, lanes],
                    sems.at[part, at],
                )
            )
    return copies


def begin(copies):
    for copy in copies:
        copy.start()


def finish(copies):
    for copy in copies:
        copy.wait()


def unit(rows):
    inverse = lax.rsqrt(jnp.mean(rows * rows, axis=-1, keepdims=True) + 1e-05)
    return rows * inverse, inverse


def attend(where, docs, gain, hidden, cot, table, *rest):
    pieces, rest = rest[:8], rest[8:]
    grads, (mix, dq_t, dkv_t), rest = rest[:8], rest[8:11], rest[11:]
    (w_q, w_kv, w_o, normed, normed_t, cot_t, dm_t, q_t, k_t, v_t, k_n, v_n) = rest[:12]
    (mix_t, dk_t, dv_t, bias, out, sems, out_sems) = rest[12:]
    copy_q, copy_kv, copy_o = assembly(where, pieces, w_q, w_kv, w_o, sems)
    begin(copy_o)
    begin(copy_q)
    begin(copy_kv)

    @pl.loop(0, TOKENS // 128)
    def _(step):
        at = pl.ds(pl.multiple_of(step * 128, 128), 128)
        value = (unit(hidden[at, :].astype(F32))[0] * gain[...]).astype(BF)
        normed[at, :] = value
        normed_t[:, at] = value.T
        cot_t[:, at] = cot[at, :].T

    for b in range(TOKENS // SEQ):
        places_q = lax.broadcasted_iota(jnp.int32, (1, SEQ), 1)
        places_s = lax.broadcasted_iota(jnp.int32, (SEQ, 1), 0)
        doc_q, doc_s, bound = jnp.zeros_like(places_q), jnp.zeros_like(places_s), 0
        for j in range(4):
            bound = bound + docs[b, j]
            doc_q = doc_q + (places_q >= bound).astype(jnp.int32)
            doc_s = doc_s + (places_s >= bound).astype(jnp.int32)
        allowed = jnp.logical_and(doc_q == doc_s, places_s <= places_q)
        bias[b] = jnp.where(allowed, 0.0, BLOCKED)

    finish(copy_o)
    for n in range(4):
        columns = w_o[:, :, :, pl.ds(n * 256, 256)].reshape(D, 256)
        dm_t[pl.ds(n * 256, 256), :] = dot(cot[...], columns).astype(BF).T

    cos, sin = table[0], table[1]
    finish(copy_q)
    for n in range(4):
        rows = w_q[pl.ds(n * 4, 4)].reshape(256, D)
        value = dot(rows, normed_t[...]) * 0.125
        for h in range(4):
            a, b = value[h * HD : h * HD + HALF], value[h * HD + HALF : (h + 1) * HD]
            q_t[pl.ds(n * 256 + h * HD, HALF), :] = (a * cos - b * sin).astype(BF)
            q_t[pl.ds(n * 256 + h * HD + HALF, HALF), :] = (a * sin + b * cos).astype(BF)
    finish(copy_kv)
    for n in range(4):
        rows = w_kv[pl.ds(n * 4, 4)].reshape(128, D)
        value = dot(rows, normed_t[...]).reshape(8, 2, 8, TOKENS)
        keys = value[:, 0].reshape(HD, TOKENS)
        a, b = keys[:HALF], keys[HALF:]
        keys = jnp.concatenate([a * cos - b * sin, a * sin + b * cos]).astype(BF)
        values = value[:, 1].reshape(HD, TOKENS).astype(BF)
        k_t[n] = keys
        v_t[n] = values
        k_n[n] = keys.T
        v_n[n] = values.T

    @pl.loop(0, 8)
    def _(step):
        head = lax.rem(step, 4)
        b = step // 4
        at = pl.ds(pl.multiple_of(b * SEQ, SEQ), SEQ)
        keys_n, values_n = k_n[head, at, :], v_n[head, at, :]
        keys_t, values_t = k_t[head, :, at], v_t[head, :, at]
        cos_b, sin_b = table[0, :, 0:SEQ] * 0.125, table[1, :, 0:SEQ] * 0.125
        d_keys = jnp.zeros((SEQ, HD), F32)
        d_values = jnp.zeros((SEQ, HD), F32)
        blank = jnp.zeros((128, 128), BF)
        for h in range(GROUP):
            rows = pl.ds(pl.multiple_of(head * 256 + h * HD, HD), HD)
            query = q_t[rows, at]
            d_mixed = dm_t[rows, at]
            scores = dot(keys_n, query)
            d_prob = dot(values_n, d_mixed)
            probs, d_scores = [], []
            for length, columns in ((128, slice(0, 128)), (256, slice(128, 256))):
                weight = jnp.exp(scores[:length, columns] + bias[b, pl.ds(0, length), columns])
                prob = weight * (1.0 / jnp.sum(weight, axis=0, keepdims=True))
                back = d_prob[:length, columns]
                inner = jnp.sum(prob * back, axis=0, keepdims=True)
                probs.append(prob.astype(BF))
                d_scores.append((prob * (back - inner)).astype(BF))
            prob = jnp.concatenate([jnp.concatenate([probs[0], blank]), probs[1]], axis=1)
            d_score = jnp.concatenate([jnp.concatenate([d_scores[0], blank]), d_scores[1]], axis=1)
            mix_t[rows, at] = dot(values_t, prob).astype(BF)
            value = dot(keys_t, d_score)
            a, c = value[:HALF], value[HALF:]
            dq_t[rows, at] = jnp.concatenate(
                [a * cos_b + c * sin_b, c * cos_b - a * sin_b]
            ).astype(BF)
            d_keys = d_keys + dot(d_score, query.T)
            d_values = d_values + dot(prob, d_mixed.T)
        value = d_keys.T
        a, c = value[:HALF], value[HALF:]
        cos_b, sin_b = table[0, :, 0:SEQ], table[1, :, 0:SEQ]
        dk_t[head, :, at] = jnp.concatenate([a * cos_b + c * sin_b, c * cos_b - a * sin_b])
        dv_t[head, :, at] = d_values.T

    for n in range(4):
        keys = dk_t[n].reshape(8, 1, 8, TOKENS)
        values = dv_t[n].reshape(8, 1, 8, TOKENS)
        both = jnp.concatenate([keys, values], axis=1).reshape(128, TOKENS)
        dkv_t[pl.ds(n * 128, 128), :] = both.astype(BF)
        mix[:, pl.ds(n * 256, 256)] = mix_t[pl.ds(n * 256, 256), :].T

    c, xl, y = where[0], where[1], where[2]
    for n in range(4):
        lanes = pl.ds(n * 256, 256)
        places = []
        for node in (2 * n, 2 * n + 1):
            places.append((lax.rem(node % 4 - y + 4, 4), lax.rem(node // 4 - xl + 2, 2)))
        for left, right, start, count in (
            (dq_t, normed, 0, 32),
            (dkv_t, normed, 32, 16),
            (cot_t, mix, 48, 32),
        ):
            size = left.shape[0] // 2
            for half in range(2):
                value = dot(left[pl.ds(half * size, size), :], right[:, lanes]).astype(BF)
                value = value.reshape(8, 2, count, 256)
                for core in range(2):
                    c_rel = lax.rem(core - c + 2, 2)
                    for i, (y_rel, xl_rel) in enumerate(places):
                        out[c_rel, y_rel, xl_rel, pl.ds(half * 8, 8), pl.ds(start, count), :] = (
                            value[:, core, :, i * 128 : (i + 1) * 128]
                        )
    copies = [
        pltpu.make_async_copy(out.at[at // 4, at % 4], grads[at], out_sems.at[at])
        for at in range(8)
    ]
    begin(copies)
    finish(copies)


def close(where, gain, hidden, cot, mix, dq_t, dkv_t, *rest):
    pieces, (output, grad_hidden), rest = rest[:8], rest[8:10], rest[10:]
    w_q, w_kv, w_o, dq, dkv, d_normed, sems = rest
    copy_q, copy_kv, copy_o = assembly(where, pieces, w_q, w_kv, w_o, sems)
    begin(copy_o)
    begin(copy_q)
    begin(copy_kv)
    for n in range(4):
        dq[:, pl.ds(n * 256, 256)] = dq_t[pl.ds(n * 256, 256), :].T
        dkv[:, pl.ds(n * 128, 128)] = dkv_t[pl.ds(n * 128, 128), :].T
    finish(copy_o)
    for n in range(4):
        lanes = pl.ds(n * 256, 256)
        rows = w_o[pl.ds(n * 4, 4)].reshape(256, D)
        value = lax.dot_general(
            mix[...], rows, (((1,), (1,)), ((), ())), preferred_element_type=F32
        )
        output[:, lanes] = (hidden[:, lanes].astype(F32) + value).astype(BF)
    finish(copy_q)
    finish(copy_kv)
    for n in range(4):
        lanes = pl.ds(n * 256, 256)
        value = dot(dq[...], w_q[:, :, :, lanes].reshape(D, 256))
        d_normed[:, lanes] = value + dot(dkv[...], w_kv[:, :, :, lanes].reshape(2 * KV, 256))

    @pl.loop(0, TOKENS // 64)
    def _(step):
        at = pl.ds(pl.multiple_of(step * 64, 64), 64)
        unit_rows, inverse = unit(hidden[at, :].astype(F32))
        d_unit = d_normed[at, :] * gain[...]
        middle = jnp.mean(d_unit * unit_rows, axis=-1, keepdims=True)
        grad_hidden[at, :] = (
            cot[at, :].astype(F32) + inverse * (d_unit - unit_rows * middle)
        ).astype(BF)


SMEM = pl.BlockSpec(memory_space=pltpu.SMEM)
VMEM = pl.BlockSpec(memory_space=pltpu.VMEM)
ANY = pl.BlockSpec(memory_space=pl.ANY)
PIECE = jax.ShapeDtypeStruct((2, CHIPS, ROWS, 128), BF)


def scratch(*shape, dtype=BF):
    return pltpu.VMEM(shape, dtype)


def weights_scratch():
    return [
        scratch(CHIPS, 2, 32, D),
        scratch(CHIPS, 2, 16, D),
        scratch(CHIPS, 2, 32, D),
    ]


def local(hidden, norm_gain, w_query, w_key, w_value, w_out, doc_lengths, cotangent):
    block = jnp.concatenate([w_query.T, w_key.T, w_value.T, w_out.T], axis=0)
    pieces = gather_blocks(block)
    where = jnp.stack([lax.axis_index(name) for name in ("c", "xl", "y")])
    gain = norm_gain.reshape(1, D)
    table = jnp.asarray(tables())
    shapes = [
        jax.ShapeDtypeStruct((TOKENS, D), BF),
        jax.ShapeDtypeStruct((D, TOKENS), BF),
        jax.ShapeDtypeStruct((2 * KV, TOKENS), BF),
    ]
    results = pl.pallas_call(
        attend,
        name="attend",
        out_shape=[PIECE] * 8 + shapes,
        in_specs=[SMEM, SMEM] + [VMEM] * 4 + [ANY] * 8,
        out_specs=[ANY] * 8 + [VMEM] * 3,
        scratch_shapes=weights_scratch()
        + [
            scratch(TOKENS, D),
            scratch(D, TOKENS),
            scratch(D, TOKENS),
            scratch(D, TOKENS),
            scratch(D, TOKENS),
            scratch(4, HD, TOKENS),
            scratch(4, HD, TOKENS),
            scratch(4, TOKENS, HD),
            scratch(4, TOKENS, HD),
            scratch(D, TOKENS),
            scratch(4, HD, TOKENS, dtype=F32),
            scratch(4, HD, TOKENS, dtype=F32),
            scratch(2, SEQ, SEQ, dtype=F32),
            scratch(2, 4, 2, CHIPS, ROWS, 128),
            pltpu.SemaphoreType.DMA((3, 16)),
            pltpu.SemaphoreType.DMA((8,)),
        ],
        compiler_params=pltpu.CompilerParams(vmem_limit_bytes=VMEM_BYTES),
        cost_estimate=pl.CostEstimate(
            flops=7 * 10**9, bytes_accessed=20 * 10**6, transcendentals=2 * 10**6
        ),
    )(where, doc_lengths, gain, hidden, cotangent, table, *pieces)
    grads, (mix, dq_t, dkv_t) = results[:8], results[8:]
    output, grad_hidden = pl.pallas_call(
        close,
        name="close",
        out_shape=[jax.ShapeDtypeStruct((TOKENS, D), BF)] * 2,
        in_specs=[SMEM] + [VMEM] * 6 + [ANY] * 8,
        out_specs=[VMEM] * 2,
        scratch_shapes=weights_scratch()
        + [
            scratch(TOKENS, D),
            scratch(TOKENS, 2 * KV),
            scratch(TOKENS, D, dtype=F32),
            pltpu.SemaphoreType.DMA((3, 16)),
        ],
        compiler_params=pltpu.CompilerParams(vmem_limit_bytes=VMEM_BYTES),
        cost_estimate=pl.CostEstimate(
            flops=3 * 10**9, bytes_accessed=15 * 10**6, transcendentals=0
        ),
    )(where, gain, hidden, cotangent, mix, dq_t, dkv_t, *pieces)
    owned = scatter_blocks(grads)
    return (
        output,
        grad_hidden,
        owned[:32].T,
        owned[32:40].T,
        owned[40:48].T,
        owned[48:].T,
    )


def solution(mesh):
    wide = jax.sharding.Mesh(mesh.devices.reshape(SIZES), AXES)
    dp, node = ("xh", "z", "c"), ("xl", "y")
    tokens, weight = P(AXES, None), P(node, dp)
    return jax.shard_map(
        local,
        mesh=wide,
        in_specs=(tokens, P(), weight, weight, weight, weight, tokens, tokens),
        out_specs=(tokens, tokens, weight, weight, weight, weight),
        check_vma=False,
    )
```

```python
import itertools

import jax
import jax.numpy as jnp
import numpy as np
from jax import lax
from jax.experimental import pallas as pl
from jax.experimental.pallas import tpu as pltpu
from jax.sharding import PartitionSpec as P

HD = 64
HALF = 32
SEQ = 256
D = 1024
KV = 256
GROUP = 4
TOKENS = 512

AXES = ("xh", "z", "c", "xl", "y")
X = ("xh", "xl")
SIZES = (2, 8, 2, 2, 4)
ROWS = 80
BF = jnp.bfloat16
F32 = jnp.float32
VMEM_BYTES = 48 * 1024 * 1024
BLOCKED = -1e30


def tables():
    frequency = 500000.0 ** (-2.0 * np.arange(HALF) / HD)
    angles = np.tile(np.arange(SEQ), TOKENS // SEQ)[None, :] * frequency[:, None]
    return np.stack([np.cos(angles), np.sin(angles)]).astype(np.float32)


def dot(left, right):
    return jnp.dot(left, right, preferred_element_type=F32)


def flat(xh, z, c, xl, y):
    return (((xh * 8 + z) * 2 + c) * 2 + xl) * 4 + y


def shift(block, along_x, step):
    pairs = []
    for x, z, c, y in itertools.product(range(4), range(8), range(2), range(4)):
        from_x, from_y = ((x + step) % 4, y) if c == along_x else (x, (y + step) % 4)
        source = flat(from_x // 2, z, c, from_x % 2, from_y)
        pairs.append((source, flat(x // 2, z, c, x % 2, y)))
    return lax.ppermute(block, AXES, pairs)


def swap(block):
    return lax.ppermute(block, "c", [(0, 1), (1, 0)])


def gather_blocks(block):
    mine = lax.all_to_all(jnp.broadcast_to(block[None], (8, ROWS, 128)), "z", 0, 0, tiled=True)
    first = jnp.stack([mine] + [shift(mine, 0, step) for step in (1, 2, 3)])
    pieces = [first] + [shift(first, 1, step) for step in (1, 2, 3)]
    return pieces + [swap(piece) for piece in pieces]


def scatter_blocks(pieces):
    summed = [
        (pieces[i].astype(F32) + swap(pieces[4 + i]).astype(F32)).astype(BF) for i in range(4)
    ]
    for along_x in (1, 0):
        total = summed[0].astype(F32)
        for step in (1, 2, 3):
            total = total + shift(summed[step], along_x, -step).astype(F32)
        summed = total.astype(BF)
    parts = lax.all_to_all(summed, "z", 0, 0, tiled=True)
    return jnp.sum(parts.astype(F32), axis=0)


def assembly(where, pieces, w_q, w_kv, w_o, sems):
    c, x, y = where[0], where[1], where[2]
    copies = ([], [], [])
    for at in range(32):
        c_rel, second, first = at // 16, (at // 4) % 4, at % 4
        core = lax.rem(c + c_rel, 2)
        chip_x = lax.rem(x + first + core * (second - first), 4)
        chip_y = lax.rem(y + second + core * (first - second), 4)
        high, node = chip_x // 2, lax.rem(chip_x, 2) * 4 + chip_y
        lanes = pl.ds(pl.multiple_of(node * 128, 128), 128)
        source = pieces[c_rel * 4 + second].at[first]
        for part, (target, start, count) in enumerate(
            ((w_q, 0, 32), (w_kv, 32, 16), (w_o, 48, 32))
        ):
            copies[part].append(
                pltpu.make_async_copy(
                    source.at[:, pl.ds(start, count), :],
                    target.at[high, :, core, :, lanes],
                    sems.at[part, at],
                )
            )
    return copies


def begin(copies):
    for copy in copies:
        copy.start()


def finish(copies):
    for copy in copies:
        copy.wait()


def unit(rows):
    inverse = lax.rsqrt(jnp.mean(rows * rows, axis=-1, keepdims=True) + 1e-05)
    return rows * inverse, inverse


def attend(where, docs, gain, hidden, cot, table, *rest):
    pieces, rest = rest[:8], rest[8:]
    grads, (mix, dq_t, dkv_t), rest = rest[:8], rest[8:11], rest[11:]
    (w_q, w_kv, w_o, normed, normed_t, cot_t, dm_t, q_t, k_t, v_t, k_n, v_n) = rest[:12]
    (mix_t, dk_t, dv_t, bias, out, sems, out_sems) = rest[12:]
    copy_q, copy_kv, copy_o = assembly(where, pieces, w_q, w_kv, w_o, sems)
    begin(copy_o)
    begin(copy_q)
    begin(copy_kv)

    @pl.loop(0, TOKENS // 128)
    def _(step):
        at = pl.ds(pl.multiple_of(step * 128, 128), 128)
        value = (unit(hidden[at, :].astype(F32))[0] * gain[...]).astype(BF)
        normed[at, :] = value
        normed_t[:, at] = value.T
        cot_t[:, at] = cot[at, :].T

    for b in range(TOKENS // SEQ):
        places_q = lax.broadcasted_iota(jnp.int32, (1, SEQ), 1)
        places_s = lax.broadcasted_iota(jnp.int32, (SEQ, 1), 0)
        doc_q, doc_s, bound = jnp.zeros_like(places_q), jnp.zeros_like(places_s), 0
        for j in range(4):
            bound = bound + docs[b, j]
            doc_q = doc_q + (places_q >= bound).astype(jnp.int32)
            doc_s = doc_s + (places_s >= bound).astype(jnp.int32)
        allowed = jnp.logical_and(doc_q == doc_s, places_s <= places_q)
        bias[b] = jnp.where(allowed, 0.0, BLOCKED)

    finish(copy_o)
    for n in range(4):
        columns = w_o[:, :, :, :, pl.ds(n * 256, 256)].reshape(D, 256)
        dm_t[pl.ds(n * 256, 256), :] = dot(cot[...], columns).astype(BF).T

    cos, sin = table[0], table[1]
    finish(copy_q)
    for n in range(4):
        rows = w_q[n // 2, pl.ds(n % 2 * 4, 4)].reshape(256, D)
        value = dot(rows, normed_t[...]) * 0.125
        for h in range(4):
            a, b = value[h * HD : h * HD + HALF], value[h * HD + HALF : (h + 1) * HD]
            q_t[pl.ds(n * 256 + h * HD, HALF), :] = (a * cos - b * sin).astype(BF)
            q_t[pl.ds(n * 256 + h * HD + HALF, HALF), :] = (a * sin + b * cos).astype(BF)
    finish(copy_kv)
    for n in range(4):
        rows = w_kv[n // 2, pl.ds(n % 2 * 4, 4)].reshape(128, D)
        value = dot(rows, normed_t[...]).reshape(8, 2, 8, TOKENS)
        keys = value[:, 0].reshape(HD, TOKENS)
        a, b = keys[:HALF], keys[HALF:]
        keys = jnp.concatenate([a * cos - b * sin, a * sin + b * cos]).astype(BF)
        values = value[:, 1].reshape(HD, TOKENS).astype(BF)
        k_t[n] = keys
        v_t[n] = values
        k_n[n] = keys.T
        v_n[n] = values.T

    @pl.loop(0, 8)
    def _(step):
        head = lax.rem(step, 4)
        b = step // 4
        at = pl.ds(pl.multiple_of(b * SEQ, SEQ), SEQ)
        keys_n, values_n = k_n[head, at, :], v_n[head, at, :]
        keys_t, values_t = k_t[head, :, at], v_t[head, :, at]
        cos_b, sin_b = table[0, :, 0:SEQ] * 0.125, table[1, :, 0:SEQ] * 0.125
        d_keys = jnp.zeros((SEQ, HD), F32)
        d_values = jnp.zeros((SEQ, HD), F32)
        blank = jnp.zeros((128, 128), BF)
        for h in range(GROUP):
            rows = pl.ds(pl.multiple_of(head * 256 + h * HD, HD), HD)
            query = q_t[rows, at]
            d_mixed = dm_t[rows, at]
            scores = dot(keys_n, query)
            d_prob = dot(values_n, d_mixed)
            probs, d_scores = [], []
            for length, columns in ((128, slice(0, 128)), (256, slice(128, 256))):
                weight = jnp.exp(scores[:length, columns] + bias[b, pl.ds(0, length), columns])
                prob = weight * (1.0 / jnp.sum(weight, axis=0, keepdims=True))
                back = d_prob[:length, columns]
                inner = jnp.sum(prob * back, axis=0, keepdims=True)
                probs.append(prob.astype(BF))
                d_scores.append((prob * (back - inner)).astype(BF))
            prob = jnp.concatenate([jnp.concatenate([probs[0], blank]), probs[1]], axis=1)
            d_score = jnp.concatenate([jnp.concatenate([d_scores[0], blank]), d_scores[1]], axis=1)
            mix_t[rows, at] = dot(values_t, prob).astype(BF)
            value = dot(keys_t, d_score)
            a, c = value[:HALF], value[HALF:]
            dq_t[rows, at] = jnp.concatenate(
                [a * cos_b + c * sin_b, c * cos_b - a * sin_b]
            ).astype(BF)
            d_keys = d_keys + dot(d_score, query.T)
            d_values = d_values + dot(prob, d_mixed.T)
        value = d_keys.T
        a, c = value[:HALF], value[HALF:]
        cos_b, sin_b = table[0, :, 0:SEQ], table[1, :, 0:SEQ]
        dk_t[head, :, at] = jnp.concatenate([a * cos_b + c * sin_b, c * cos_b - a * sin_b])
        dv_t[head, :, at] = d_values.T

    for n in range(4):
        keys = dk_t[n].reshape(8, 1, 8, TOKENS)
        values = dv_t[n].reshape(8, 1, 8, TOKENS)
        both = jnp.concatenate([keys, values], axis=1).reshape(128, TOKENS)
        dkv_t[pl.ds(n * 128, 128), :] = both.astype(BF)
        mix[:, pl.ds(n * 256, 256)] = mix_t[pl.ds(n * 256, 256), :].T

    c, x, y = where[0], where[1], where[2]
    for n in range(4):
        lanes = pl.ds(n * 256, 256)
        for left, right, start, count in (
            (dq_t, normed, 0, 32),
            (dkv_t, normed, 32, 16),
            (cot_t, mix, 48, 32),
        ):
            size = left.shape[0] // 2
            for high in range(2):
                value = dot(left[pl.ds(high * size, size), :], right[:, lanes]).astype(BF)
                value = value.reshape(8, 2, count, 256)
                x_rel = lax.rem(high * 2 + n // 2 - x + 4, 4)
                for i in range(2):
                    y_rel = lax.rem(n % 2 * 2 + i - y + 4, 4)
                    for core, (second, first) in enumerate(((y_rel, x_rel), (x_rel, y_rel))):
                        c_rel = lax.rem(core - c + 2, 2)
                        out[c_rel, second, first, :, pl.ds(start, count), :] = (
                            value[:, core, :, i * 128 : (i + 1) * 128]
                        )
    copies = [
        pltpu.make_async_copy(out.at[at // 4, at % 4], grads[at], out_sems.at[at])
        for at in range(8)
    ]
    begin(copies)
    finish(copies)


def close(where, gain, hidden, cot, mix, dq_t, dkv_t, *rest):
    pieces, (output, grad_hidden), rest = rest[:8], rest[8:10], rest[10:]
    w_q, w_kv, w_o, dq, dkv, d_normed, sems = rest
    copy_q, copy_kv, copy_o = assembly(where, pieces, w_q, w_kv, w_o, sems)
    begin(copy_o)
    begin(copy_q)
    begin(copy_kv)
    for n in range(4):
        dq[:, pl.ds(n * 256, 256)] = dq_t[pl.ds(n * 256, 256), :].T
        dkv[:, pl.ds(n * 128, 128)] = dkv_t[pl.ds(n * 128, 128), :].T
    finish(copy_o)
    for n in range(4):
        lanes = pl.ds(n * 256, 256)
        rows = w_o[n // 2, pl.ds(n % 2 * 4, 4)].reshape(256, D)
        value = lax.dot_general(
            mix[...], rows, (((1,), (1,)), ((), ())), preferred_element_type=F32
        )
        output[:, lanes] = (hidden[:, lanes].astype(F32) + value).astype(BF)
    finish(copy_q)
    finish(copy_kv)
    for n in range(4):
        lanes = pl.ds(n * 256, 256)
        value = dot(dq[...], w_q[:, :, :, :, lanes].reshape(D, 256))
        d_normed[:, lanes] = value + dot(dkv[...], w_kv[:, :, :, :, lanes].reshape(2 * KV, 256))

    @pl.loop(0, TOKENS // 64)
    def _(step):
        at = pl.ds(pl.multiple_of(step * 64, 64), 64)
        unit_rows, inverse = unit(hidden[at, :].astype(F32))
        d_unit = d_normed[at, :] * gain[...]
        middle = jnp.mean(d_unit * unit_rows, axis=-1, keepdims=True)
        grad_hidden[at, :] = (
            cot[at, :].astype(F32) + inverse * (d_unit - unit_rows * middle)
        ).astype(BF)


SMEM = pl.BlockSpec(memory_space=pltpu.SMEM)
VMEM = pl.BlockSpec(memory_space=pltpu.VMEM)
ANY = pl.BlockSpec(memory_space=pl.ANY)
PIECE = jax.ShapeDtypeStruct((4, 8, ROWS, 128), BF)


def scratch(*shape, dtype=BF):
    return pltpu.VMEM(shape, dtype)


def weights_scratch():
    return [
        scratch(2, 8, 2, 32, D),
        scratch(2, 8, 2, 16, D),
        scratch(2, 8, 2, 32, D),
    ]


def local(hidden, norm_gain, w_query, w_key, w_value, w_out, doc_lengths, cotangent):
    block = jnp.concatenate([w_query.T, w_key.T, w_value.T, w_out.T], axis=0)
    pieces = gather_blocks(block)
    where = jnp.stack([lax.axis_index(name) for name in ("c", X, "y")])
    gain = norm_gain.reshape(1, D)
    table = jnp.asarray(tables())
    shapes = [
        jax.ShapeDtypeStruct((TOKENS, D), BF),
        jax.ShapeDtypeStruct((D, TOKENS), BF),
        jax.ShapeDtypeStruct((2 * KV, TOKENS), BF),
    ]
    results = pl.pallas_call(
        attend,
        name="attend",
        out_shape=[PIECE] * 8 + shapes,
        in_specs=[SMEM, SMEM] + [VMEM] * 4 + [ANY] * 8,
        out_specs=[ANY] * 8 + [VMEM] * 3,
        scratch_shapes=weights_scratch()
        + [
            scratch(TOKENS, D),
            scratch(D, TOKENS),
            scratch(D, TOKENS),
            scratch(D, TOKENS),
            scratch(D, TOKENS),
            scratch(4, HD, TOKENS),
            scratch(4, HD, TOKENS),
            scratch(4, TOKENS, HD),
            scratch(4, TOKENS, HD),
            scratch(D, TOKENS),
            scratch(4, HD, TOKENS, dtype=F32),
            scratch(4, HD, TOKENS, dtype=F32),
            scratch(2, SEQ, SEQ, dtype=F32),
            scratch(2, 4, 4, 8, ROWS, 128),
            pltpu.SemaphoreType.DMA((3, 32)),
            pltpu.SemaphoreType.DMA((8,)),
        ],
        compiler_params=pltpu.CompilerParams(vmem_limit_bytes=VMEM_BYTES),
        cost_estimate=pl.CostEstimate(
            flops=7 * 10**9, bytes_accessed=20 * 10**6, transcendentals=2 * 10**6
        ),
    )(where, doc_lengths, gain, hidden, cotangent, table, *pieces)
    grads, (mix, dq_t, dkv_t) = results[:8], results[8:]
    output, grad_hidden = pl.pallas_call(
        close,
        name="close",
        out_shape=[jax.ShapeDtypeStruct((TOKENS, D), BF)] * 2,
        in_specs=[SMEM] + [VMEM] * 6 + [ANY] * 8,
        out_specs=[VMEM] * 2,
        scratch_shapes=weights_scratch()
        + [
            scratch(TOKENS, D),
            scratch(TOKENS, 2 * KV),
            scratch(TOKENS, D, dtype=F32),
            pltpu.SemaphoreType.DMA((3, 32)),
        ],
        compiler_params=pltpu.CompilerParams(vmem_limit_bytes=VMEM_BYTES),
        cost_estimate=pl.CostEstimate(
            flops=3 * 10**9, bytes_accessed=15 * 10**6, transcendentals=0
        ),
    )(where, gain, hidden, cotangent, mix, dq_t, dkv_t, *pieces)
    owned = scatter_blocks(grads)
    return (
        output,
        grad_hidden,
        owned[:32].T,
        owned[32:40].T,
        owned[40:48].T,
        owned[48:].T,
    )


def solution(mesh):
    wide = jax.sharding.Mesh(mesh.devices.reshape(SIZES), AXES)
    dp, node = ("xh", "z", "c"), ("xl", "y")
    tokens, weight = P(AXES, None), P(node, dp)
    return jax.shard_map(
        local,
        mesh=wide,
        in_specs=(tokens, P(), weight, weight, weight, weight, tokens, tokens),
        out_specs=(tokens, tokens, weight, weight, weight, weight),
        check_vma=False,
    )
```

```python
import itertools

import jax
import jax.numpy as jnp
import numpy as np
from jax import lax
from jax.experimental import pallas as pl
from jax.experimental.pallas import tpu as pltpu
from jax.sharding import PartitionSpec as P

HD = 64
HALF = 32
SEQ = 256
D = 1024
KV = 256
GROUP = 4
TOKENS = 512

AXES = ("xh", "z", "c", "xl", "y")
X = ("xh", "xl")
SIZES = (2, 8, 2, 2, 4)
ROWS = 80
BF = jnp.bfloat16
F32 = jnp.float32
VMEM_BYTES = 40 * 1024 * 1024
BLOCKED = -1e30


def tables():
    frequency = 500000.0 ** (-2.0 * np.arange(HALF) / HD)
    angles = np.tile(np.arange(SEQ), TOKENS // SEQ)[None, :] * frequency[:, None]
    return np.stack([np.cos(angles), np.sin(angles)]).astype(np.float32)


def dot(left, right):
    return jnp.dot(left, right, preferred_element_type=F32)


def flat(xh, z, c, xl, y):
    return (((xh * 8 + z) * 2 + c) * 2 + xl) * 4 + y


def shift(block, along_x, step):
    pairs = []
    for x, z, c, y in itertools.product(range(4), range(8), range(2), range(4)):
        from_x, from_y = ((x + step) % 4, y) if c == along_x else (x, (y + step) % 4)
        source = flat(from_x // 2, z, c, from_x % 2, from_y)
        pairs.append((source, flat(x // 2, z, c, x % 2, y)))
    return lax.ppermute(block, AXES, pairs)


def swap(block):
    return lax.ppermute(block, "c", [(0, 1), (1, 0)])


def gather_blocks(block):
    mine = lax.all_to_all(jnp.broadcast_to(block[None], (8, ROWS, 128)), "z", 0, 0, tiled=True)
    first = jnp.stack([mine] + [shift(mine, 0, step) for step in (1, 2, 3)])
    pieces = [first] + [shift(first, 1, step) for step in (1, 2, 3)]
    return pieces + [swap(piece) for piece in pieces]


def scatter_blocks(pieces, beside):
    summed = [
        (pieces[i].astype(F32) + swap(pieces[4 + i]).astype(F32)).astype(BF) for i in range(4)
    ]
    for along_x in (1, 0):
        total = summed[0].astype(F32)
        for step in (1, 2, 3):
            total = total + shift(summed[step], along_x, -step).astype(F32)
        summed, beside = lax.optimization_barrier((total.astype(BF), beside))
    parts = lax.all_to_all(summed, "z", 0, 0, tiled=True)
    return jnp.sum(parts.astype(F32), axis=0), beside


def assembly(where, pieces, w_q, w_kv, w_o, sems):
    c, x, y = where[0], where[1], where[2]
    copies = ([], [], [])
    for at in range(32):
        c_rel, second, first = at // 16, (at // 4) % 4, at % 4
        core = lax.rem(c + c_rel, 2)
        chip_x = lax.rem(x + first + core * (second - first), 4)
        chip_y = lax.rem(y + second + core * (first - second), 4)
        high, node = chip_x // 2, lax.rem(chip_x, 2) * 4 + chip_y
        lanes = pl.ds(pl.multiple_of(node * 128, 128), 128)
        source = pieces[c_rel * 4 + second].at[first]
        for part, (target, start, count) in enumerate(
            ((w_q, 0, 32), (w_kv, 32, 16), (w_o, 48, 32))
        ):
            copies[part].append(
                pltpu.make_async_copy(
                    source.at[:, pl.ds(start, count), :],
                    target.at[high, :, core, :, lanes],
                    sems.at[part, at],
                )
            )
    return copies


def begin(copies):
    for copy in copies:
        copy.start()


def finish(copies):
    for copy in copies:
        copy.wait()


def unit(rows):
    inverse = lax.rsqrt(jnp.mean(rows * rows, axis=-1, keepdims=True) + 1e-05)
    return rows * inverse, inverse


def attend(where, docs, gain, hidden, cot, table, *rest):
    pieces, rest = rest[:8], rest[8:]
    grads, (mix, dq_t, dkv_t), rest = rest[:8], rest[8:11], rest[11:]
    (w_q, w_kv, w_o, normed, normed_t, cot_t, dm_t, q_t, k_t, v_t, k_n, v_n) = rest[:12]
    (mix_t, dk_t, dv_t, bias, out, sems) = rest[12:]
    copy_q, copy_kv, copy_o = assembly(where, pieces, w_q, w_kv, w_o, sems)
    begin(copy_o)
    begin(copy_q)
    begin(copy_kv)

    @pl.loop(0, TOKENS // 128)
    def _(step):
        at = pl.ds(pl.multiple_of(step * 128, 128), 128)
        value = (unit(hidden[at, :].astype(F32))[0] * gain[...]).astype(BF)
        normed[at, :] = value
        normed_t[:, at] = value.T
        cot_t[:, at] = cot[at, :].T

    for b in range(TOKENS // SEQ):
        places_q = lax.broadcasted_iota(jnp.int32, (1, SEQ), 1)
        places_s = lax.broadcasted_iota(jnp.int32, (SEQ, 1), 0)
        doc_q, doc_s, bound = jnp.zeros_like(places_q), jnp.zeros_like(places_s), 0
        for j in range(4):
            bound = bound + docs[b, j]
            doc_q = doc_q + (places_q >= bound).astype(jnp.int32)
            doc_s = doc_s + (places_s >= bound).astype(jnp.int32)
        allowed = jnp.logical_and(doc_q == doc_s, places_s <= places_q)
        bias[b] = jnp.where(allowed, 0.0, BLOCKED)

    finish(copy_o)
    for n in range(4):
        columns = w_o[:, :, :, :, pl.ds(n * 256, 256)].reshape(D, 256)
        dm_t[pl.ds(n * 256, 256), :] = dot(cot[...], columns).astype(BF).T

    cos, sin = table[0], table[1]
    finish(copy_q)
    for n in range(4):
        rows = w_q[n // 2, pl.ds(n % 2 * 4, 4)].reshape(256, D)
        value = dot(rows, normed_t[...]) * 0.125
        for h in range(4):
            a, b = value[h * HD : h * HD + HALF], value[h * HD + HALF : (h + 1) * HD]
            q_t[pl.ds(n * 256 + h * HD, HALF), :] = (a * cos - b * sin).astype(BF)
            q_t[pl.ds(n * 256 + h * HD + HALF, HALF), :] = (a * sin + b * cos).astype(BF)
    finish(copy_kv)
    for n in range(4):
        rows = w_kv[n // 2, pl.ds(n % 2 * 4, 4)].reshape(128, D)
        value = dot(rows, normed_t[...]).reshape(8, 2, 8, TOKENS)
        keys = value[:, 0].reshape(HD, TOKENS)
        a, b = keys[:HALF], keys[HALF:]
        keys = jnp.concatenate([a * cos - b * sin, a * sin + b * cos]).astype(BF)
        values = value[:, 1].reshape(HD, TOKENS).astype(BF)
        k_t[n] = keys
        v_t[n] = values
        k_n[n] = keys.T
        v_n[n] = values.T

    @pl.loop(0, 8, unroll=2)
    def _(step):
        head = lax.rem(step, 4)
        b = step // 4
        at = pl.ds(pl.multiple_of(b * SEQ, SEQ), SEQ)
        keys_n, values_n = k_n[head, at, :], v_n[head, at, :]
        keys_t, values_t = k_t[head, :, at], v_t[head, :, at]
        cos_b, sin_b = table[0, :, 0:SEQ] * 0.125, table[1, :, 0:SEQ] * 0.125
        d_keys = jnp.zeros((SEQ, HD), F32)
        d_values = jnp.zeros((SEQ, HD), F32)
        blank = jnp.zeros((128, 128), BF)
        places = [pl.ds(pl.multiple_of(head * 256 + h * HD, HD), HD) for h in range(GROUP)]
        queries = [q_t[rows, at] for rows in places]
        d_mixeds = [dm_t[rows, at] for rows in places]
        scores = [dot(keys_n, query) for query in queries]
        d_probs = [dot(values_n, d_mixed) for d_mixed in d_mixeds]
        both = []
        for h in range(GROUP):
            probs, d_scores = [], []
            for length, columns in ((128, slice(0, 128)), (256, slice(128, 256))):
                weight = jnp.exp(scores[h][:length, columns] + bias[b, pl.ds(0, length), columns])
                prob = weight * (1.0 / jnp.sum(weight, axis=0, keepdims=True))
                back = d_probs[h][:length, columns]
                inner = jnp.sum(prob * back, axis=0, keepdims=True)
                probs.append(prob.astype(BF))
                d_scores.append((prob * (back - inner)).astype(BF))
            both.append([
                jnp.concatenate([jnp.concatenate([part[0], blank]), part[1]], axis=1)
                for part in (probs, d_scores)
            ])
        for h in range(GROUP):
            prob, d_score = both[h]
            rows = places[h]
            mix_t[rows, at] = dot(values_t, prob).astype(BF)
            value = dot(keys_t, d_score)
            a, c = value[:HALF], value[HALF:]
            dq_t[rows, at] = jnp.concatenate(
                [a * cos_b + c * sin_b, c * cos_b - a * sin_b]
            ).astype(BF)
            d_keys = d_keys + dot(d_score, queries[h].T)
            d_values = d_values + dot(prob, d_mixeds[h].T)
        value = d_keys.T
        a, c = value[:HALF], value[HALF:]
        cos_b, sin_b = table[0, :, 0:SEQ], table[1, :, 0:SEQ]
        dk_t[head, :, at] = jnp.concatenate([a * cos_b + c * sin_b, c * cos_b - a * sin_b])
        dv_t[head, :, at] = d_values.T

    for n in range(4):
        keys = dk_t[n].reshape(8, 1, 8, TOKENS)
        values = dv_t[n].reshape(8, 1, 8, TOKENS)
        both = jnp.concatenate([keys, values], axis=1).reshape(128, TOKENS)
        dkv_t[pl.ds(n * 128, 128), :] = both.astype(BF)
        mix[:, pl.ds(n * 256, 256)] = mix_t[pl.ds(n * 256, 256), :].T

    for n in range(4):
        lanes = pl.ds(n * 256, 256)
        for left, right, start, count in (
            (dq_t, normed, 0, 32),
            (dkv_t, normed, 32, 16),
            (cot_t, mix, 48, 32),
        ):
            size = left.shape[0] // 2
            for high in range(2):
                value = dot(left[pl.ds(high * size, size), :], right[:, lanes]).astype(BF)
                value = value.reshape(8, 2, count, 256)
                for core, i in itertools.product(range(2), range(2)):
                    out[core, high * 2 + n // 2, n % 2 * 2 + i, :, pl.ds(start, count), :] = (
                        value[:, core, :, i * 128 : (i + 1) * 128]
                    )
    c, x, y = where[0], where[1], where[2]
    for at in range(32):
        c_rel, second, first = at // 16, (at // 4) % 4, at % 4
        core = lax.rem(c + c_rel, 2)
        chip_x = lax.rem(x + first + core * (second - first), 4)
        chip_y = lax.rem(y + second + core * (first - second), 4)
        grads[c_rel * 4 + second][first] = out[core, chip_x, chip_y]


def close(where, gain, hidden, cot, mix, dq_t, dkv_t, *rest):
    pieces, (output, grad_hidden), rest = rest[:8], rest[8:10], rest[10:]
    w_q, w_kv, w_o, dq, dkv, d_normed, sems = rest
    copy_q, copy_kv, copy_o = assembly(where, pieces, w_q, w_kv, w_o, sems)
    begin(copy_o)
    begin(copy_q)
    begin(copy_kv)
    for n in range(4):
        dq[:, pl.ds(n * 256, 256)] = dq_t[pl.ds(n * 256, 256), :].T
        dkv[:, pl.ds(n * 128, 128)] = dkv_t[pl.ds(n * 128, 128), :].T
    finish(copy_o)
    for n in range(4):
        lanes = pl.ds(n * 256, 256)
        rows = w_o[n // 2, pl.ds(n % 2 * 4, 4)].reshape(256, D)
        value = lax.dot_general(
            mix[...], rows, (((1,), (1,)), ((), ())), preferred_element_type=F32
        )
        output[:, lanes] = (hidden[:, lanes].astype(F32) + value).astype(BF)
    finish(copy_q)
    finish(copy_kv)
    for n in range(4):
        lanes = pl.ds(n * 256, 256)
        value = dot(dq[...], w_q[:, :, :, :, lanes].reshape(D, 256))
        d_normed[:, lanes] = value + dot(dkv[...], w_kv[:, :, :, :, lanes].reshape(2 * KV, 256))

    @pl.loop(0, TOKENS // 64)
    def _(step):
        at = pl.ds(pl.multiple_of(step * 64, 64), 64)
        unit_rows, inverse = unit(hidden[at, :].astype(F32))
        d_unit = d_normed[at, :] * gain[...]
        middle = jnp.mean(d_unit * unit_rows, axis=-1, keepdims=True)
        grad_hidden[at, :] = (
            cot[at, :].astype(F32) + inverse * (d_unit - unit_rows * middle)
        ).astype(BF)


SMEM = pl.BlockSpec(memory_space=pltpu.SMEM)
VMEM = pl.BlockSpec(memory_space=pltpu.VMEM)
ANY = pl.BlockSpec(memory_space=pl.ANY)
PIECE = jax.ShapeDtypeStruct((4, 8, ROWS, 128), BF)


def scratch(*shape, dtype=BF):
    return pltpu.VMEM(shape, dtype)


def weights_scratch():
    return [
        scratch(2, 8, 2, 32, D),
        scratch(2, 8, 2, 16, D),
        scratch(2, 8, 2, 32, D),
    ]


def local(hidden, norm_gain, w_query, w_key, w_value, w_out, doc_lengths, cotangent):
    block = jnp.concatenate([w_query.T, w_key.T, w_value.T, w_out.T], axis=0)
    pieces = gather_blocks(block)
    where = jnp.stack([lax.axis_index(name) for name in ("c", X, "y")])
    gain = norm_gain.reshape(1, D)
    table = jnp.asarray(tables())
    shapes = [
        jax.ShapeDtypeStruct((TOKENS, D), BF),
        jax.ShapeDtypeStruct((D, TOKENS), BF),
        jax.ShapeDtypeStruct((2 * KV, TOKENS), BF),
    ]
    results = pl.pallas_call(
        attend,
        name="attend",
        out_shape=[PIECE] * 8 + shapes,
        in_specs=[SMEM, SMEM] + [VMEM] * 4 + [ANY] * 8,
        out_specs=[VMEM] * 11,
        scratch_shapes=weights_scratch()
        + [
            scratch(TOKENS, D),
            scratch(D, TOKENS),
            scratch(D, TOKENS),
            scratch(D, TOKENS),
            scratch(D, TOKENS),
            scratch(4, HD, TOKENS),
            scratch(4, HD, TOKENS),
            scratch(4, TOKENS, HD),
            scratch(4, TOKENS, HD),
            scratch(D, TOKENS),
            scratch(4, HD, TOKENS, dtype=F32),
            scratch(4, HD, TOKENS, dtype=F32),
            scratch(2, SEQ, SEQ, dtype=F32),
            scratch(2, 4, 4, 8, ROWS, 128),
            pltpu.SemaphoreType.DMA((3, 32)),
        ],
        compiler_params=pltpu.CompilerParams(vmem_limit_bytes=VMEM_BYTES),
        cost_estimate=pl.CostEstimate(
            flops=7 * 10**9, bytes_accessed=20 * 10**6, transcendentals=2 * 10**6
        ),
    )(where, doc_lengths, gain, hidden, cotangent, table, *pieces)
    grads, (mix, dq_t, dkv_t) = results[:8], results[8:]
    beside = pl.pallas_call(
        close,
        name="close",
        out_shape=[jax.ShapeDtypeStruct((TOKENS, D), BF)] * 2,
        in_specs=[SMEM] + [VMEM] * 6 + [ANY] * 8,
        out_specs=[VMEM] * 2,
        scratch_shapes=weights_scratch()
        + [
            scratch(TOKENS, D),
            scratch(TOKENS, 2 * KV),
            scratch(TOKENS, D, dtype=F32),
            pltpu.SemaphoreType.DMA((3, 32)),
        ],
        compiler_params=pltpu.CompilerParams(vmem_limit_bytes=VMEM_BYTES),
        cost_estimate=pl.CostEstimate(
            flops=3 * 10**9, bytes_accessed=15 * 10**6, transcendentals=0
        ),
    )(where, gain, hidden, cotangent, mix, dq_t, dkv_t, *pieces)
    owned, (output, grad_hidden) = scatter_blocks(grads, tuple(beside))
    return (
        output,
        grad_hidden,
        owned[:32].T,
        owned[32:40].T,
        owned[40:48].T,
        owned[48:].T,
    )


def solution(mesh):
    wide = jax.sharding.Mesh(mesh.devices.reshape(SIZES), AXES)
    dp, node = ("xh", "z", "c"), ("xl", "y")
    tokens, weight = P(AXES, None), P(node, dp)
    return jax.shard_map(
        local,
        mesh=wide,
        in_specs=(tokens, P(), weight, weight, weight, weight, tokens, tokens),
        out_specs=(tokens, tokens, weight, weight, weight, weight),
        check_vma=False,
    )
```

```python
import itertools

import jax
import jax.numpy as jnp
import numpy as np
from jax import lax
from jax.experimental import pallas as pl
from jax.experimental.pallas import tpu as pltpu
from jax.sharding import PartitionSpec as P

HD = 64
HALF = 32
SEQ = 256
D = 1024
KV = 256
GROUP = 4
TOKENS = 512

AXES = ("xh", "z", "c", "xl", "y")
X = ("xh", "xl")
SIZES = (2, 8, 2, 2, 4)
ROWS = 80
BF = jnp.bfloat16
F32 = jnp.float32
VMEM_BYTES = 40 * 1024 * 1024
BLOCKED = -1e30


def tables():
    frequency = 500000.0 ** (-2.0 * np.arange(HALF) / HD)
    angles = np.tile(np.arange(SEQ), TOKENS // SEQ)[None, :] * frequency[:, None]
    return np.stack([np.cos(angles), np.sin(angles)]).astype(np.float32)


def dot(left, right):
    return jnp.dot(left, right, preferred_element_type=F32)


def flat(xh, z, c, xl, y):
    return (((xh * 8 + z) * 2 + c) * 2 + xl) * 4 + y


def shift(block, along_x, step):
    pairs = []
    for x, z, c, y in itertools.product(range(4), range(8), range(2), range(4)):
        from_x, from_y = ((x + step) % 4, y) if c == along_x else (x, (y + step) % 4)
        source = flat(from_x // 2, z, c, from_x % 2, from_y)
        pairs.append((source, flat(x // 2, z, c, x % 2, y)))
    return lax.ppermute(block, AXES, pairs)


def swap(block):
    return lax.ppermute(block, "c", [(0, 1), (1, 0)])


def gather_blocks(block, ready):
    mine = lax.all_to_all(jnp.broadcast_to(block[None], (8, ROWS, 128)), "z", 0, 0, tiled=True)
    first = jnp.stack([mine] + [shift(mine, 0, step) for step in (1, 2, 3)])
    pieces = [first] + [shift(first, 1, step) for step in (1, 2, 3)]
    pieces[3], ready = lax.optimization_barrier((pieces[3], ready))
    return pieces + [swap(piece) for piece in pieces], ready


def scatter_blocks(pieces, beside):
    summed = [
        (pieces[i].astype(F32) + swap(pieces[4 + i]).astype(F32)).astype(BF) for i in range(4)
    ]
    for along_x in (1, 0):
        total = summed[0].astype(F32)
        for step in (1, 2, 3):
            total = total + shift(summed[step], along_x, -step).astype(F32)
        summed, beside = lax.optimization_barrier((total.astype(BF), beside))
    parts = lax.all_to_all(summed, "z", 0, 0, tiled=True)
    return jnp.sum(parts.astype(F32), axis=0), beside


def assembly(where, pieces, w_q, w_kv, w_o, sems):
    c, x, y = where[0], where[1], where[2]
    copies = ([], [], [])
    for at in range(32):
        c_rel, second, first = at // 16, (at // 4) % 4, at % 4
        core = lax.rem(c + c_rel, 2)
        chip_x = lax.rem(x + first + core * (second - first), 4)
        chip_y = lax.rem(y + second + core * (first - second), 4)
        high, node = chip_x // 2, lax.rem(chip_x, 2) * 4 + chip_y
        lanes = pl.ds(pl.multiple_of(node * 128, 128), 128)
        source = pieces[c_rel * 4 + second].at[first]
        for part, (target, start, count) in enumerate(
            ((w_q, 0, 32), (w_kv, 32, 16), (w_o, 48, 32))
        ):
            copies[part].append(
                pltpu.make_async_copy(
                    source.at[:, pl.ds(start, count), :],
                    target.at[high, :, core, :, lanes],
                    sems.at[part, at],
                )
            )
    return copies


def assemble(where, pieces, w_q, w_kv, w_o):
    c, x, y = where[0], where[1], where[2]
    for at in range(32):
        c_rel, second, first = at // 16, (at // 4) % 4, at % 4
        core = lax.rem(c + c_rel, 2)
        chip_x = lax.rem(x + first + core * (second - first), 4)
        chip_y = lax.rem(y + second + core * (first - second), 4)
        high, node = chip_x // 2, lax.rem(chip_x, 2) * 4 + chip_y
        lanes = pl.ds(pl.multiple_of(node * 128, 128), 128)
        piece = pieces[c_rel * 4 + second]
        w_q[high, :, core, :, lanes] = piece[first, :, 0:32, :]
        w_kv[high, :, core, :, lanes] = piece[first, :, 32:48, :]
        w_o[high, :, core, :, lanes] = piece[first, :, 48:80, :]


def begin(copies):
    for copy in copies:
        copy.start()


def finish(copies):
    for copy in copies:
        copy.wait()


def unit(rows):
    inverse = lax.rsqrt(jnp.mean(rows * rows, axis=-1, keepdims=True) + 1e-05)
    return rows * inverse, inverse


def prepare(docs, gain, hidden, cot, normed, normed_t, cot_t, bias):
    @pl.loop(0, TOKENS // 128)
    def _(step):
        at = pl.ds(pl.multiple_of(step * 128, 128), 128)
        value = (unit(hidden[at, :].astype(F32))[0] * gain[...]).astype(BF)
        normed[at, :] = value
        normed_t[:, at] = value.T
        cot_t[:, at] = cot[at, :].T

    for b in range(TOKENS // SEQ):
        places_q = lax.broadcasted_iota(jnp.int32, (1, SEQ), 1)
        places_s = lax.broadcasted_iota(jnp.int32, (SEQ, 1), 0)
        doc_q, doc_s, bound = jnp.zeros_like(places_q), jnp.zeros_like(places_s), 0
        for j in range(4):
            bound = bound + docs[b, j]
            doc_q = doc_q + (places_q >= bound).astype(jnp.int32)
            doc_s = doc_s + (places_s >= bound).astype(jnp.int32)
        allowed = jnp.logical_and(doc_q == doc_s, places_s <= places_q)
        bias[b] = jnp.where(allowed, 0.0, BLOCKED)


def attend(where, cot, table, normed, normed_t, cot_t, bias, *rest):
    pieces, rest = rest[:8], rest[8:]
    grads, (mix, dq_t, dkv_t), rest = rest[:8], rest[8:11], rest[11:]
    (w_q, w_kv, w_o, dm_t, q_t, k_t, v_t, k_n, v_n) = rest[:9]
    (mix_t, dk_t, dv_t, out) = rest[9:]

    assemble(where, pieces, w_q, w_kv, w_o)
    for n in range(4):
        columns = w_o[:, :, :, :, pl.ds(n * 256, 256)].reshape(D, 256)
        dm_t[pl.ds(n * 256, 256), :] = dot(cot[...], columns).astype(BF).T

    cos, sin = table[0], table[1]
    for n in range(4):
        rows = w_q[n // 2, pl.ds(n % 2 * 4, 4)].reshape(256, D)
        value = dot(rows, normed_t[...]) * 0.125
        for h in range(4):
            a, b = value[h * HD : h * HD + HALF], value[h * HD + HALF : (h + 1) * HD]
            q_t[pl.ds(n * 256 + h * HD, HALF), :] = (a * cos - b * sin).astype(BF)
            q_t[pl.ds(n * 256 + h * HD + HALF, HALF), :] = (a * sin + b * cos).astype(BF)
    for n in range(4):
        rows = w_kv[n // 2, pl.ds(n % 2 * 4, 4)].reshape(128, D)
        value = dot(rows, normed_t[...]).reshape(8, 2, 8, TOKENS)
        keys = value[:, 0].reshape(HD, TOKENS)
        a, b = keys[:HALF], keys[HALF:]
        keys = jnp.concatenate([a * cos - b * sin, a * sin + b * cos]).astype(BF)
        values = value[:, 1].reshape(HD, TOKENS).astype(BF)
        k_t[n] = keys
        v_t[n] = values
        k_n[n] = keys.T
        v_n[n] = values.T

    @pl.loop(0, 8, unroll=2)
    def _(step):
        head = lax.rem(step, 4)
        b = step // 4
        at = pl.ds(pl.multiple_of(b * SEQ, SEQ), SEQ)
        keys_n, values_n = k_n[head, at, :], v_n[head, at, :]
        keys_t, values_t = k_t[head, :, at], v_t[head, :, at]
        cos_b, sin_b = table[0, :, 0:SEQ] * 0.125, table[1, :, 0:SEQ] * 0.125
        d_keys = jnp.zeros((SEQ, HD), F32)
        d_values = jnp.zeros((SEQ, HD), F32)
        blank = jnp.zeros((128, 128), BF)
        places = [pl.ds(pl.multiple_of(head * 256 + h * HD, HD), HD) for h in range(GROUP)]
        queries = [q_t[rows, at] for rows in places]
        d_mixeds = [dm_t[rows, at] for rows in places]
        scores = [dot(keys_n, query) for query in queries]
        d_probs = [dot(values_n, d_mixed) for d_mixed in d_mixeds]
        both = []
        for h in range(GROUP):
            probs, d_scores = [], []
            for length, columns in ((128, slice(0, 128)), (256, slice(128, 256))):
                weight = jnp.exp(scores[h][:length, columns] + bias[b, pl.ds(0, length), columns])
                prob = weight * (1.0 / jnp.sum(weight, axis=0, keepdims=True))
                back = d_probs[h][:length, columns]
                inner = jnp.sum(prob * back, axis=0, keepdims=True)
                probs.append(prob.astype(BF))
                d_scores.append((prob * (back - inner)).astype(BF))
            both.append([
                jnp.concatenate([jnp.concatenate([part[0], blank]), part[1]], axis=1)
                for part in (probs, d_scores)
            ])
        for h in range(GROUP):
            prob, d_score = both[h]
            rows = places[h]
            mix_t[rows, at] = dot(values_t, prob).astype(BF)
            value = dot(keys_t, d_score)
            a, c = value[:HALF], value[HALF:]
            dq_t[rows, at] = jnp.concatenate(
                [a * cos_b + c * sin_b, c * cos_b - a * sin_b]
            ).astype(BF)
            d_keys = d_keys + dot(d_score, queries[h].T)
            d_values = d_values + dot(prob, d_mixeds[h].T)
        value = d_keys.T
        a, c = value[:HALF], value[HALF:]
        cos_b, sin_b = table[0, :, 0:SEQ], table[1, :, 0:SEQ]
        dk_t[head, :, at] = jnp.concatenate([a * cos_b + c * sin_b, c * cos_b - a * sin_b])
        dv_t[head, :, at] = d_values.T

    for n in range(4):
        keys = dk_t[n].reshape(8, 1, 8, TOKENS)
        values = dv_t[n].reshape(8, 1, 8, TOKENS)
        both = jnp.concatenate([keys, values], axis=1).reshape(128, TOKENS)
        dkv_t[pl.ds(n * 128, 128), :] = both.astype(BF)
        mix[:, pl.ds(n * 256, 256)] = mix_t[pl.ds(n * 256, 256), :].T

    for n in range(4):
        lanes = pl.ds(n * 256, 256)
        for left, right, start, count in (
            (dq_t, normed, 0, 32),
            (dkv_t, normed, 32, 16),
            (cot_t, mix, 48, 32),
        ):
            size = left.shape[0] // 2
            for high in range(2):
                value = dot(left[pl.ds(high * size, size), :], right[:, lanes]).astype(BF)
                value = value.reshape(8, 2, count, 256)
                for core, i in itertools.product(range(2), range(2)):
                    out[core, high * 2 + n // 2, n % 2 * 2 + i, :, pl.ds(start, count), :] = (
                        value[:, core, :, i * 128 : (i + 1) * 128]
                    )
    c, x, y = where[0], where[1], where[2]
    for at in range(32):
        c_rel, second, first = at // 16, (at // 4) % 4, at % 4
        core = lax.rem(c + c_rel, 2)
        chip_x = lax.rem(x + first + core * (second - first), 4)
        chip_y = lax.rem(y + second + core * (first - second), 4)
        grads[c_rel * 4 + second][first] = out[core, chip_x, chip_y]


def close(where, gain, hidden, cot, mix, dq_t, dkv_t, *rest):
    pieces, (output, grad_hidden), rest = rest[:8], rest[8:10], rest[10:]
    w_q, w_kv, w_o, dq, dkv, d_normed, sems = rest
    copy_q, copy_kv, copy_o = assembly(where, pieces, w_q, w_kv, w_o, sems)
    begin(copy_o)
    begin(copy_q)
    begin(copy_kv)
    for n in range(4):
        dq[:, pl.ds(n * 256, 256)] = dq_t[pl.ds(n * 256, 256), :].T
        dkv[:, pl.ds(n * 128, 128)] = dkv_t[pl.ds(n * 128, 128), :].T
    finish(copy_o)
    for n in range(4):
        lanes = pl.ds(n * 256, 256)
        rows = w_o[n // 2, pl.ds(n % 2 * 4, 4)].reshape(256, D)
        value = lax.dot_general(
            mix[...], rows, (((1,), (1,)), ((), ())), preferred_element_type=F32
        )
        output[:, lanes] = (hidden[:, lanes].astype(F32) + value).astype(BF)
    finish(copy_q)
    finish(copy_kv)
    for n in range(4):
        lanes = pl.ds(n * 256, 256)
        value = dot(dq[...], w_q[:, :, :, :, lanes].reshape(D, 256))
        d_normed[:, lanes] = value + dot(dkv[...], w_kv[:, :, :, :, lanes].reshape(2 * KV, 256))

    @pl.loop(0, TOKENS // 64)
    def _(step):
        at = pl.ds(pl.multiple_of(step * 64, 64), 64)
        unit_rows, inverse = unit(hidden[at, :].astype(F32))
        d_unit = d_normed[at, :] * gain[...]
        middle = jnp.mean(d_unit * unit_rows, axis=-1, keepdims=True)
        grad_hidden[at, :] = (
            cot[at, :].astype(F32) + inverse * (d_unit - unit_rows * middle)
        ).astype(BF)


SMEM = pl.BlockSpec(memory_space=pltpu.SMEM)
VMEM = pl.BlockSpec(memory_space=pltpu.VMEM)
ANY = pl.BlockSpec(memory_space=pl.ANY)
PIECE = jax.ShapeDtypeStruct((4, 8, ROWS, 128), BF)


def scratch(*shape, dtype=BF):
    return pltpu.VMEM(shape, dtype)


def weights_scratch():
    return [
        scratch(2, 8, 2, 32, D),
        scratch(2, 8, 2, 16, D),
        scratch(2, 8, 2, 32, D),
    ]


def local(hidden, norm_gain, w_query, w_key, w_value, w_out, doc_lengths, cotangent):
    block = jnp.concatenate([w_query.T, w_key.T, w_value.T, w_out.T], axis=0)
    where = jnp.stack([lax.axis_index(name) for name in ("c", X, "y")])
    gain = norm_gain.reshape(1, D)
    table = jnp.asarray(tables())
    shapes = [
        jax.ShapeDtypeStruct((TOKENS, D), BF),
        jax.ShapeDtypeStruct((D, TOKENS), BF),
        jax.ShapeDtypeStruct((2 * KV, TOKENS), BF),
    ]
    ready = pl.pallas_call(
        prepare,
        name="prepare",
        out_shape=[
            pltpu.VMEM((TOKENS, D), BF),
            pltpu.VMEM((D, TOKENS), BF),
            pltpu.VMEM((D, TOKENS), BF),
            pltpu.VMEM((2, SEQ, SEQ), F32),
        ],
        in_specs=[SMEM, VMEM, VMEM, VMEM],
        out_specs=[VMEM] * 4,
        compiler_params=pltpu.CompilerParams(vmem_limit_bytes=VMEM_BYTES // 2),
    )(doc_lengths, gain, hidden, cotangent)
    pieces, ready = gather_blocks(block, tuple(ready))
    results = pl.pallas_call(
        attend,
        name="attend",
        out_shape=[PIECE] * 8 + shapes,
        in_specs=[SMEM] + [VMEM] * 14,
        out_specs=[VMEM] * 11,
        scratch_shapes=weights_scratch()
        + [
            scratch(D, TOKENS),
            scratch(D, TOKENS),
            scratch(4, HD, TOKENS),
            scratch(4, HD, TOKENS),
            scratch(4, TOKENS, HD),
            scratch(4, TOKENS, HD),
            scratch(D, TOKENS),
            scratch(4, HD, TOKENS, dtype=F32),
            scratch(4, HD, TOKENS, dtype=F32),
            scratch(2, 4, 4, 8, ROWS, 128),
        ],
        compiler_params=pltpu.CompilerParams(vmem_limit_bytes=VMEM_BYTES),
        cost_estimate=pl.CostEstimate(
            flops=7 * 10**9, bytes_accessed=20 * 10**6, transcendentals=2 * 10**6
        ),
    )(where, cotangent, table, *ready, *[pltpu.with_memory_space_constraint(p, pltpu.VMEM) for p in pieces])
    grads, (mix, dq_t, dkv_t) = results[:8], results[8:]
    beside = pl.pallas_call(
        close,
        name="close",
        out_shape=[jax.ShapeDtypeStruct((TOKENS, D), BF)] * 2,
        in_specs=[SMEM] + [VMEM] * 6 + [ANY] * 8,
        out_specs=[VMEM] * 2,
        scratch_shapes=weights_scratch()
        + [
            scratch(TOKENS, D),
            scratch(TOKENS, 2 * KV),
            scratch(TOKENS, D, dtype=F32),
            pltpu.SemaphoreType.DMA((3, 32)),
        ],
        compiler_params=pltpu.CompilerParams(vmem_limit_bytes=VMEM_BYTES),
        cost_estimate=pl.CostEstimate(
            flops=3 * 10**9, bytes_accessed=15 * 10**6, transcendentals=0
        ),
    )(where, gain, hidden, cotangent, mix, dq_t, dkv_t, *pieces)
    owned, (output, grad_hidden) = scatter_blocks(grads, tuple(beside))
    return (
        output,
        grad_hidden,
        owned[:32].T,
        owned[32:40].T,
        owned[40:48].T,
        owned[48:].T,
    )


def solution(mesh):
    wide = jax.sharding.Mesh(mesh.devices.reshape(SIZES), AXES)
    dp, node = ("xh", "z", "c"), ("xl", "y")
    tokens, weight = P(AXES, None), P(node, dp)
    return jax.shard_map(
        local,
        mesh=wide,
        in_specs=(tokens, P(), weight, weight, weight, weight, tokens, tokens),
        out_specs=(tokens, tokens, weight, weight, weight, weight),
        check_vma=False,
    )
```

```python
import itertools

import jax
import jax.numpy as jnp
import numpy as np
from jax import lax
from jax.experimental import pallas as pl
from jax.experimental.pallas import tpu as pltpu
from jax.sharding import PartitionSpec as P

HD = 64
HALF = 32
SEQ = 256
D = 1024
KV = 256
GROUP = 4
TOKENS = 512

AXES = ("xh", "z", "c", "xl", "y")
X = ("xh", "xl")
SIZES = (2, 8, 2, 2, 4)
ROWS = 80
BF = jnp.bfloat16
F32 = jnp.float32
VMEM_BYTES = 40 * 1024 * 1024
BLOCKED = -1e30


def tables():
    frequency = 500000.0 ** (-2.0 * np.arange(HALF) / HD)
    angles = np.tile(np.arange(SEQ), TOKENS // SEQ)[None, :] * frequency[:, None]
    return np.stack([np.cos(angles), np.sin(angles)]).astype(np.float32)


def dot(left, right):
    return jnp.dot(left, right, preferred_element_type=F32)


def flat(xh, z, c, xl, y):
    return (((xh * 8 + z) * 2 + c) * 2 + xl) * 4 + y


def shift(block, along_x, step):
    pairs = []
    for x, z, c, y in itertools.product(range(4), range(8), range(2), range(4)):
        from_x, from_y = ((x + step) % 4, y) if c == along_x else (x, (y + step) % 4)
        source = flat(from_x // 2, z, c, from_x % 2, from_y)
        pairs.append((source, flat(x // 2, z, c, x % 2, y)))
    return lax.ppermute(block, AXES, pairs)


def swap(block):
    return lax.ppermute(block, "c", [(0, 1), (1, 0)])


def gather_blocks(block, ready):
    mine = lax.all_to_all(jnp.broadcast_to(block[None], (8, ROWS, 128)), "z", 0, 0, tiled=True)
    first = jnp.stack([mine] + [shift(mine, 0, step) for step in (1, 2, 3)])
    pieces = [first] + [shift(first, 1, step) for step in (1, 2, 3)]
    pieces[3], mask = lax.optimization_barrier((pieces[3], ready[3]))
    ready = (*ready[:3], mask)
    return pieces + [swap(piece) for piece in pieces], ready


def scatter_blocks(pieces, beside):
    summed = [
        (pieces[i].astype(F32) + swap(pieces[4 + i]).astype(F32)).astype(BF) for i in range(4)
    ]
    for along_x in (1, 0):
        total = summed[0].astype(F32)
        for step in (1, 2, 3):
            total = total + shift(summed[step], along_x, -step).astype(F32)
        summed, beside = lax.optimization_barrier((total.astype(BF), beside))
    parts = lax.all_to_all(summed, "z", 0, 0, tiled=True)
    return jnp.sum(parts.astype(F32), axis=0), beside


def assembly(where, pieces, w_q, w_kv, w_o, sems):
    c, x, y = where[0], where[1], where[2]
    copies = ([], [], [])
    for at in range(32):
        c_rel, second, first = at // 16, (at // 4) % 4, at % 4
        core = lax.rem(c + c_rel, 2)
        chip_x = lax.rem(x + first + core * (second - first), 4)
        chip_y = lax.rem(y + second + core * (first - second), 4)
        high, node = chip_x // 2, lax.rem(chip_x, 2) * 4 + chip_y
        lanes = pl.ds(pl.multiple_of(node * 128, 128), 128)
        source = pieces[c_rel * 4 + second].at[first]
        for part, (target, start, count) in enumerate(
            ((w_q, 0, 32), (w_kv, 32, 16), (w_o, 48, 32))
        ):
            copies[part].append(
                pltpu.make_async_copy(
                    source.at[:, pl.ds(start, count), :],
                    target.at[high, :, core, :, lanes],
                    sems.at[part, at],
                )
            )
    return copies


def assemble(where, pieces, w_q, w_kv, w_o):
    c, x, y = where[0], where[1], where[2]
    for at in range(32):
        c_rel, second, first = at // 16, (at // 4) % 4, at % 4
        core = lax.rem(c + c_rel, 2)
        chip_x = lax.rem(x + first + core * (second - first), 4)
        chip_y = lax.rem(y + second + core * (first - second), 4)
        high, node = chip_x // 2, lax.rem(chip_x, 2) * 4 + chip_y
        lanes = pl.ds(pl.multiple_of(node * 128, 128), 128)
        piece = pieces[c_rel * 4 + second]
        w_q[high, :, core, :, lanes] = piece[first, :, 0:32, :]
        w_kv[high, :, core, :, lanes] = piece[first, :, 32:48, :]
        w_o[high, :, core, :, lanes] = piece[first, :, 48:80, :]


def begin(copies):
    for copy in copies:
        copy.start()


def finish(copies):
    for copy in copies:
        copy.wait()


def unit(rows):
    inverse = lax.rsqrt(jnp.mean(rows * rows, axis=-1, keepdims=True) + 1e-05)
    return rows * inverse, inverse


def prepare(docs, gain, hidden, cot, normed, normed_t, cot_t, bias):
    @pl.loop(0, TOKENS // 128)
    def _(step):
        at = pl.ds(pl.multiple_of(step * 128, 128), 128)
        value = (unit(hidden[at, :].astype(F32))[0] * gain[...]).astype(BF)
        normed[at, :] = value
        normed_t[:, at] = value.T
        cot_t[:, at] = cot[at, :].T

    for b in range(TOKENS // SEQ):
        places_q = lax.broadcasted_iota(jnp.int32, (1, SEQ), 1)
        places_s = lax.broadcasted_iota(jnp.int32, (SEQ, 1), 0)
        doc_q, doc_s, bound = jnp.zeros_like(places_q), jnp.zeros_like(places_s), 0
        for j in range(4):
            bound = bound + docs[b, j]
            doc_q = doc_q + (places_q >= bound).astype(jnp.int32)
            doc_s = doc_s + (places_s >= bound).astype(jnp.int32)
        allowed = jnp.logical_and(doc_q == doc_s, places_s <= places_q)
        bias[b] = jnp.where(allowed, 0.0, BLOCKED)


def attend(where, cot, table, normed, normed_t, cot_t, bias, *rest):
    pieces, rest = rest[:8], rest[8:]
    grads, (mix, dq_t, dkv_t), rest = rest[:8], rest[8:11], rest[11:]
    (w_q, w_kv, w_o, dm_t, q_t, k_t, v_t, k_n, v_n) = rest[:9]
    (mix_t, dk_t, dv_t, out) = rest[9:]

    assemble(where, pieces, w_q, w_kv, w_o)
    for n in range(4):
        columns = w_o[:, :, :, :, pl.ds(n * 256, 256)].reshape(D, 256)
        dm_t[pl.ds(n * 256, 256), :] = dot(cot[...], columns).astype(BF).T

    cos, sin = table[0], table[1]
    for n in range(4):
        rows = w_q[n // 2, pl.ds(n % 2 * 4, 4)].reshape(256, D)
        value = dot(rows, normed_t[...]) * 0.125
        for h in range(4):
            a, b = value[h * HD : h * HD + HALF], value[h * HD + HALF : (h + 1) * HD]
            q_t[pl.ds(n * 256 + h * HD, HALF), :] = (a * cos - b * sin).astype(BF)
            q_t[pl.ds(n * 256 + h * HD + HALF, HALF), :] = (a * sin + b * cos).astype(BF)
    for n in range(4):
        rows = w_kv[n // 2, pl.ds(n % 2 * 4, 4)].reshape(128, D)
        value = dot(rows, normed_t[...]).reshape(8, 2, 8, TOKENS)
        keys = value[:, 0].reshape(HD, TOKENS)
        a, b = keys[:HALF], keys[HALF:]
        keys = jnp.concatenate([a * cos - b * sin, a * sin + b * cos]).astype(BF)
        values = value[:, 1].reshape(HD, TOKENS).astype(BF)
        k_t[n] = keys
        v_t[n] = values
        k_n[n] = keys.T
        v_n[n] = values.T

    @pl.loop(0, 8, unroll=2)
    def _(step):
        head = lax.rem(step, 4)
        b = step // 4
        at = pl.ds(pl.multiple_of(b * SEQ, SEQ), SEQ)
        keys_n, values_n = k_n[head, at, :], v_n[head, at, :]
        keys_t, values_t = k_t[head, :, at], v_t[head, :, at]
        cos_b, sin_b = table[0, :, 0:SEQ] * 0.125, table[1, :, 0:SEQ] * 0.125
        d_keys = jnp.zeros((SEQ, HD), F32)
        d_values = jnp.zeros((SEQ, HD), F32)
        blank = jnp.zeros((128, 128), BF)
        places = [pl.ds(pl.multiple_of(head * 256 + h * HD, HD), HD) for h in range(GROUP)]
        queries = [q_t[rows, at] for rows in places]
        d_mixeds = [dm_t[rows, at] for rows in places]
        scores = [dot(keys_n, query) for query in queries]
        d_probs = [dot(values_n, d_mixed) for d_mixed in d_mixeds]
        both = []
        for h in range(GROUP):
            probs, d_scores = [], []
            for length, columns in ((128, slice(0, 128)), (256, slice(128, 256))):
                weight = jnp.exp(scores[h][:length, columns] + bias[b, pl.ds(0, length), columns])
                prob = weight * (1.0 / jnp.sum(weight, axis=0, keepdims=True))
                back = d_probs[h][:length, columns]
                inner = jnp.sum(prob * back, axis=0, keepdims=True)
                probs.append(prob.astype(BF))
                d_scores.append((prob * (back - inner)).astype(BF))
            both.append([
                jnp.concatenate([jnp.concatenate([part[0], blank]), part[1]], axis=1)
                for part in (probs, d_scores)
            ])
        for h in range(GROUP):
            prob, d_score = both[h]
            rows = places[h]
            mix_t[rows, at] = dot(values_t, prob).astype(BF)
            value = dot(keys_t, d_score)
            a, c = value[:HALF], value[HALF:]
            dq_t[rows, at] = jnp.concatenate(
                [a * cos_b + c * sin_b, c * cos_b - a * sin_b]
            ).astype(BF)
            d_keys = d_keys + dot(d_score, queries[h].T)
            d_values = d_values + dot(prob, d_mixeds[h].T)
        value = d_keys.T
        a, c = value[:HALF], value[HALF:]
        cos_b, sin_b = table[0, :, 0:SEQ], table[1, :, 0:SEQ]
        dk_t[head, :, at] = jnp.concatenate([a * cos_b + c * sin_b, c * cos_b - a * sin_b])
        dv_t[head, :, at] = d_values.T

    for n in range(4):
        keys = dk_t[n].reshape(8, 1, 8, TOKENS)
        values = dv_t[n].reshape(8, 1, 8, TOKENS)
        both = jnp.concatenate([keys, values], axis=1).reshape(128, TOKENS)
        dkv_t[pl.ds(n * 128, 128), :] = both.astype(BF)
        mix[:, pl.ds(n * 256, 256)] = mix_t[pl.ds(n * 256, 256), :].T

    for n in range(4):
        lanes = pl.ds(n * 256, 256)
        for left, right, start, count in (
            (dq_t, normed, 0, 32),
            (dkv_t, normed, 32, 16),
            (cot_t, mix, 48, 32),
        ):
            size = left.shape[0] // 2
            for high in range(2):
                value = dot(left[pl.ds(high * size, size), :], right[:, lanes]).astype(BF)
                value = value.reshape(8, 2, count, 256)
                for core, i in itertools.product(range(2), range(2)):
                    out[core, high * 2 + n // 2, n % 2 * 2 + i, :, pl.ds(start, count), :] = (
                        value[:, core, :, i * 128 : (i + 1) * 128]
                    )
    c, x, y = where[0], where[1], where[2]
    for at in range(32):
        c_rel, second, first = at // 16, (at // 4) % 4, at % 4
        core = lax.rem(c + c_rel, 2)
        chip_x = lax.rem(x + first + core * (second - first), 4)
        chip_y = lax.rem(y + second + core * (first - second), 4)
        grads[c_rel * 4 + second][first] = out[core, chip_x, chip_y]


def close(where, gain, hidden, cot, mix, dq_t, dkv_t, *rest):
    pieces, (output, grad_hidden), rest = rest[:8], rest[8:10], rest[10:]
    w_q, w_kv, w_o, dq, dkv, d_normed, sems = rest
    copy_q, copy_kv, copy_o = assembly(where, pieces, w_q, w_kv, w_o, sems)
    begin(copy_o)
    begin(copy_q)
    begin(copy_kv)
    for n in range(4):
        dq[:, pl.ds(n * 256, 256)] = dq_t[pl.ds(n * 256, 256), :].T
        dkv[:, pl.ds(n * 128, 128)] = dkv_t[pl.ds(n * 128, 128), :].T
    finish(copy_o)
    for n in range(4):
        lanes = pl.ds(n * 256, 256)
        rows = w_o[n // 2, pl.ds(n % 2 * 4, 4)].reshape(256, D)
        value = lax.dot_general(
            mix[...], rows, (((1,), (1,)), ((), ())), preferred_element_type=F32
        )
        output[:, lanes] = (hidden[:, lanes].astype(F32) + value).astype(BF)
    finish(copy_q)
    finish(copy_kv)
    for n in range(4):
        lanes = pl.ds(n * 256, 256)
        value = dot(dq[...], w_q[:, :, :, :, lanes].reshape(D, 256))
        d_normed[:, lanes] = value + dot(dkv[...], w_kv[:, :, :, :, lanes].reshape(2 * KV, 256))

    @pl.loop(0, TOKENS // 64)
    def _(step):
        at = pl.ds(pl.multiple_of(step * 64, 64), 64)
        unit_rows, inverse = unit(hidden[at, :].astype(F32))
        d_unit = d_normed[at, :] * gain[...]
        middle = jnp.mean(d_unit * unit_rows, axis=-1, keepdims=True)
        grad_hidden[at, :] = (
            cot[at, :].astype(F32) + inverse * (d_unit - unit_rows * middle)
        ).astype(BF)


SMEM = pl.BlockSpec(memory_space=pltpu.SMEM)
VMEM = pl.BlockSpec(memory_space=pltpu.VMEM)
ANY = pl.BlockSpec(memory_space=pl.ANY)
PIECE = jax.ShapeDtypeStruct((4, 8, ROWS, 128), BF)


def scratch(*shape, dtype=BF):
    return pltpu.VMEM(shape, dtype)


def weights_scratch():
    return [
        scratch(2, 8, 2, 32, D),
        scratch(2, 8, 2, 16, D),
        scratch(2, 8, 2, 32, D),
    ]


def local(hidden, norm_gain, w_query, w_key, w_value, w_out, doc_lengths, cotangent):
    block = jnp.concatenate([w_query.T, w_key.T, w_value.T, w_out.T], axis=0)
    where = jnp.stack([lax.axis_index(name) for name in ("c", X, "y")])
    gain = norm_gain.reshape(1, D)
    table = jnp.asarray(tables())
    shapes = [
        jax.ShapeDtypeStruct((TOKENS, D), BF),
        jax.ShapeDtypeStruct((D, TOKENS), BF),
        jax.ShapeDtypeStruct((2 * KV, TOKENS), BF),
    ]
    ready = pl.pallas_call(
        prepare,
        name="prepare",
        out_shape=[
            pltpu.VMEM((TOKENS, D), BF),
            pltpu.VMEM((D, TOKENS), BF),
            pltpu.VMEM((D, TOKENS), BF),
            pltpu.VMEM((2, SEQ, SEQ), F32),
        ],
        in_specs=[SMEM, VMEM, VMEM, VMEM],
        out_specs=[VMEM] * 4,
        compiler_params=pltpu.CompilerParams(vmem_limit_bytes=VMEM_BYTES // 2),
    )(doc_lengths, gain, hidden, cotangent)
    pieces, ready = gather_blocks(block, tuple(ready))
    results = pl.pallas_call(
        attend,
        name="attend",
        out_shape=[PIECE] * 8 + shapes,
        in_specs=[SMEM] + [VMEM] * 14,
        out_specs=[VMEM] * 11,
        scratch_shapes=weights_scratch()
        + [
            scratch(D, TOKENS),
            scratch(D, TOKENS),
            scratch(4, HD, TOKENS),
            scratch(4, HD, TOKENS),
            scratch(4, TOKENS, HD),
            scratch(4, TOKENS, HD),
            scratch(D, TOKENS),
            scratch(4, HD, TOKENS, dtype=F32),
            scratch(4, HD, TOKENS, dtype=F32),
            scratch(2, 4, 4, 8, ROWS, 128),
        ],
        compiler_params=pltpu.CompilerParams(vmem_limit_bytes=VMEM_BYTES),
        cost_estimate=pl.CostEstimate(
            flops=7 * 10**9, bytes_accessed=20 * 10**6, transcendentals=2 * 10**6
        ),
    )(where, cotangent, table, *ready, *[pltpu.with_memory_space_constraint(p, pltpu.VMEM) for p in pieces])
    grads, (mix, dq_t, dkv_t) = results[:8], results[8:]
    beside = pl.pallas_call(
        close,
        name="close",
        out_shape=[jax.ShapeDtypeStruct((TOKENS, D), BF)] * 2,
        in_specs=[SMEM] + [VMEM] * 6 + [ANY] * 8,
        out_specs=[VMEM] * 2,
        scratch_shapes=weights_scratch()
        + [
            scratch(TOKENS, D),
            scratch(TOKENS, 2 * KV),
            scratch(TOKENS, D, dtype=F32),
            pltpu.SemaphoreType.DMA((3, 32)),
        ],
        compiler_params=pltpu.CompilerParams(vmem_limit_bytes=VMEM_BYTES),
        cost_estimate=pl.CostEstimate(
            flops=3 * 10**9, bytes_accessed=15 * 10**6, transcendentals=0
        ),
    )(where, gain, hidden, cotangent, mix, dq_t, dkv_t, *pieces)
    owned, (output, grad_hidden) = scatter_blocks(grads, tuple(beside))
    return (
        output,
        grad_hidden,
        owned[:32].T,
        owned[32:40].T,
        owned[40:48].T,
        owned[48:].T,
    )


def solution(mesh):
    wide = jax.sharding.Mesh(mesh.devices.reshape(SIZES), AXES)
    dp, node = ("xh", "z", "c"), ("xl", "y")
    tokens, weight = P(AXES, None), P(node, dp)
    return jax.shard_map(
        local,
        mesh=wide,
        in_specs=(tokens, P(), weight, weight, weight, weight, tokens, tokens),
        out_specs=(tokens, tokens, weight, weight, weight, weight),
        check_vma=False,
    )
```
